32 devices in a mesh: pipe: 4 (over x, core), ulys: 8 (over z, y).
Axes of the slice: x: 2, y: 2, z: 4, core: 2. Of those that a mesh axis runs over, the one named last changes fastest.
Arguments:
- activations: bfloat16 [4, 256, 3072], P('pipe', 'ulys'), may hold values from -6 to 6
- patch_index: int32 [4], P('pipe'), may hold values from 0 to 11
- modulation: float32 [4, 3, 3072], P('pipe'), may hold values from -4 to 4
- qkv_weight: bfloat16 [4, 3072, 9216], P('pipe', None, 'ulys'), may hold values from -0.109375 to 0.109375
- out_weight: bfloat16 [4, 3072, 3072], P('pipe', 'ulys'), may hold values from -0.109375 to 0.109375
- stale_cache: bfloat16 [4, 8, 3072, 2, 384], P('pipe', 'ulys'), may hold values from -360 to 360
- id_cache: bfloat16 [4, 8, 6, 32, 2, 384], P('pipe', 'ulys'), may hold values from -360 to 360
- region_ids: int32 [4, 256], P('pipe', 'ulys'), may hold values from 0 to 6
- id_counts: int32 [4, 6], P('pipe'), may hold values from 1 to 32, as said below
Outputs:
- next_activations: bfloat16 [4, 256, 3072], P('pipe', 'ulys')
The draws below stay inside these ranges and needn't reach their ends.
Inputs may be any that keep to these rules, and one draw needn't show every extreme that they name: `id_counts`: in every section some subject has exactly 32 live identity tokens.
All inputs are finite; a program needn't handle non-finite values.
Results may differ from the reference program's by a relative error of at most 0.0117.
The reference program's roundings to bfloat16 on the way (of `hidden`, `fields` and `mixed`) count: a program that leaves them out, or rounds other values in their place, can miss the bound.
Values may be sent and summed in bfloat16 or wider, within the bound.
No kernel may reach another device: no remote copies, remote signals or barrier semaphores. Data moves between devices by JAX's collectives and lax.ppermute only.
A program may use at most 128 MiB of HBM per device.

```python
import jax
import jax.numpy as jnp
from jax import lax

D = 3072
HEADS = 24
HD = 128
HPD = 3
GROUPS = 8
KSPLIT = 1
MB = 256
PATCHES = 12
S = 3072
SUBJ = 6
IDTOK = 32
SECTIONS = 4
N_ULYS = 8


def draw_stale_cache(key, part):
    key = jax.random.fold_in(key, 11)
    shape = (SECTIONS, N_ULYS, S // KSPLIT, 2, HPD * HD)
    values = jnp.clip(jax.random.normal(key, shape, jnp.float32), -6.0, 6.0)
    return values.astype(jnp.bfloat16)


def draw_id_cache(key, part):
    key = jax.random.fold_in(key, 17)
    shape = (SECTIONS, N_ULYS, SUBJ, IDTOK // KSPLIT, 2, HPD * HD)
    values = jnp.clip(jax.random.normal(key, shape, jnp.float32), -6.0, 6.0)
    return values.astype(jnp.bfloat16)


def draw_id_counts(key, part):
    key = jax.random.fold_in(key, 23)
    first, second = jax.random.split(key)
    counts = jax.random.randint(first, (SECTIONS, SUBJ), 1, IDTOK + 1)
    chosen = jax.random.randint(second, (SECTIONS, 1), 0, SUBJ)
    hit = jnp.arange(SUBJ)[None, :] == chosen
    return jnp.where(hit, IDTOK, counts).astype(jnp.int32)


def with_ends(array, key, low, largest):
    place = [jax.random.randint(jax.random.fold_in(key, axis), (), 0, length) for axis, length in enumerate(array.shape)]
    longest = array.shape.index(max(array.shape))
    neighbour = place[:longest] + [(place[longest] + 1) % array.shape[longest]] + place[longest + 1:]
    return array.at[tuple(place)].set(low).at[tuple(neighbour)].set(largest)


def level_of(rng, shape, shards, smallest, high):
    loudness, own = 1.0, jax.random.fold_in(rng, 6)
    for dim, blocks in shards:
        steps = jnp.exp(jax.random.uniform(jax.random.fold_in(own, dim), (blocks,), jnp.float32, smallest / len(shards), high / len(shards)))
        loudness = loudness * jnp.repeat(steps, shape[dim] // blocks).reshape([-1 if axis == dim else 1 for axis in range(len(shape))])
    return loudness


def gaussian(stream_key, shape, deviation, most, cuts=(), kind=jnp.bfloat16):
    values = deviation * jax.random.normal(stream_key, shape, jnp.float32)
    if cuts:
        values = values * level_of(stream_key, shape, cuts, -0.22, 0.18)
    return jnp.clip(values, -most, most).astype(kind)


def setup_inputs(seed: int = 0) -> dict:
    key_list = jax.random.split(jax.random.key(seed), 10)
    activations = gaussian(key_list[0], (SECTIONS, MB, D), 1.0, 6.0, ((0, 4), (1, 8)))
    patch_index = with_ends(jax.random.randint(key_list[1], (SECTIONS,), 0, PATCHES), jax.random.fold_in(key_list[1], 1), 0, PATCHES - 1).astype(jnp.int32)
    modulation = gaussian(key_list[2], (SECTIONS, 3, D), 0.6, 4.0, ((0, 4),), jnp.float32)
    qkv_weight = gaussian(key_list[3], (SECTIONS, D, 3 * HEADS * HD), D ** -0.5, 0.109375, ((0, 4), (2, 8)))
    out_weight = gaussian(key_list[4], (SECTIONS, HEADS * HD, D), (HEADS * HD) ** -0.5, 0.109375, ((0, 4), (1, 8)))
    stale_cache = draw_stale_cache(jax.random.fold_in(key_list[9], 71), 0)
    id_cache = draw_id_cache(jax.random.fold_in(key_list[9], 71), 0)
    region_ids = with_ends(jax.random.randint(key_list[7], (SECTIONS, MB), 0, SUBJ + 1), jax.random.fold_in(key_list[7], 1), 0, SUBJ).astype(jnp.int32)
    id_counts = draw_id_counts(jax.random.fold_in(key_list[9], 71), 0)
    return {"activations": activations, "patch_index": patch_index, "modulation": modulation, "qkv_weight": qkv_weight, "out_weight": out_weight, "stale_cache": stale_cache, "id_cache": id_cache, "region_ids": region_ids, "id_counts": id_counts}


NEG_BIG = -1e+30

def section_pass(rows, modul, patch, qkv_w, out_w, cache, id_block, region, counts):
    lifted = rows.astype(jnp.float32)
    center = lax.optimization_barrier(jnp.mean(lifted, axis=1, keepdims=True))
    spread = lax.optimization_barrier(jnp.mean(jnp.square(lifted - center), axis=1, keepdims=True))
    normed = (lifted - center) * lax.rsqrt(spread + 1e-06)
    hidden = (normed * (1.0 + modul[1]) + modul[0]).astype(jnp.bfloat16)
    ordered = qkv_w.reshape(D, GROUPS, KSPLIT, 3, HPD, HD // KSPLIT).transpose(0, 3, 1, 4, 2, 5).reshape(D, 3 * HEADS * HD)
    fields = jnp.dot(hidden, ordered, preferred_element_type=jnp.float32).astype(jnp.bfloat16).reshape(MB, 3, HEADS, HD)
    queries = fields[:, 0].transpose(1, 0, 2)
    fresh_keys = fields[:, 1].transpose(1, 0, 2)
    fresh_values = fields[:, 2].transpose(1, 0, 2)
    stored = cache.reshape(GROUPS, KSPLIT, S // KSPLIT, 2, HPD, HD).transpose(3, 0, 4, 1, 2, 5).reshape(2, HEADS, S, HD)
    start = (patch * MB).astype(jnp.int32)
    zero = jnp.zeros((), jnp.int32)
    keys = lax.dynamic_update_slice(stored[0], fresh_keys, (zero, start, zero))
    values = lax.dynamic_update_slice(stored[1], fresh_values, (zero, start, zero))
    guests = id_block.reshape(GROUPS, KSPLIT, SUBJ, IDTOK // KSPLIT, 2, HPD, HD).transpose(4, 0, 5, 2, 1, 3, 6).reshape(2, HEADS, SUBJ * IDTOK, HD)
    slot = jnp.arange(IDTOK, dtype=jnp.int32)
    valid = slot[None, :] < counts[:, None]
    subject = jnp.arange(1, SUBJ + 1, dtype=jnp.int32)
    mask = ((region[:, None] == subject[None, :])[:, :, None] & valid[None]).reshape(MB, SUBJ * IDTOK)
    factor = HD ** (-0.5)

    def one_head(items):
        head_q, head_k, head_v, guest_k, guest_v = items
        scores = jnp.dot(head_q, head_k.T, preferred_element_type=jnp.float32) * factor
        peak = lax.optimization_barrier(jnp.max(scores, axis=1, keepdims=True))
        weights = jnp.exp(scores - peak)
        own = jnp.dot(weights.astype(jnp.bfloat16), head_v, preferred_element_type=jnp.float32) / lax.optimization_barrier(jnp.sum(weights, axis=1, keepdims=True))
        guest_scores = jnp.dot(head_q, guest_k.T, preferred_element_type=jnp.float32) * factor
        guest_peak = lax.optimization_barrier(jnp.max(jnp.where(mask, guest_scores, NEG_BIG), axis=1, keepdims=True))
        guest_weights = jnp.where(mask, jnp.exp(jnp.where(mask, guest_scores - guest_peak, 0.0)), 0.0)
        guest_total = jnp.maximum(lax.optimization_barrier(jnp.sum(guest_weights, axis=1, keepdims=True)), 1.0)
        guest = jnp.dot(guest_weights.astype(jnp.bfloat16), guest_v, preferred_element_type=jnp.float32) / guest_total
        return own + guest
    mixed = lax.map(one_head, (queries, keys, values, guests[0], guests[1]))
    mixed = mixed.transpose(1, 0, 2).reshape(MB, HEADS * HD).astype(jnp.bfloat16)
    out_ordered = out_w.reshape(GROUPS, KSPLIT, HPD, HD // KSPLIT, D).transpose(0, 2, 1, 3, 4).reshape(HEADS * HD, D)
    added = jnp.dot(mixed, out_ordered, preferred_element_type=jnp.float32)
    return (lifted + modul[2] * added).astype(jnp.bfloat16)

def reference(activations, patch_index, modulation, qkv_weight, out_weight, stale_cache, id_cache, region_ids, id_counts):
    results = []
    for section in range(SECTIONS):
        results.append(section_pass(activations[section], modulation[section], patch_index[section], qkv_weight[section], out_weight[section], stale_cache[section], id_cache[section], region_ids[section], id_counts[section]))
    return jnp.roll(jnp.stack(results), 1, axis=0)
```

```python
import functools
import math

import jax
import jax.numpy as jnp
from jax import lax
from jax.experimental import pallas as pl
from jax.experimental.pallas import tpu as pltpu
from jax.sharding import PartitionSpec as P

HD = 128
HPD = 3
GROUPS = 8
SUBJ = 6


NEG_BIG = -1e30


def as_sent(x):
    return jax.tree.map(lambda a: a.astype(jnp.bfloat16) if a.dtype == jnp.float32 else a, x)


def from_partner(x, axis, apart):
    return lax.ppermute(x, axis, [(i, i ^ 1 << apart) for i in range(lax.axis_size(axis))])


def passed_along(x, axis, by):
    size = lax.axis_size(axis)
    return lax.ppermute(x, axis, [(i, (i + by) % size) for i in range(size)])


def order_pair(mine, other, rank, level, axis):
    upper = rank // 2**level % 2
    first = jnp.where(upper == 1, other, mine)
    second = jnp.where(upper == 1, mine, other)
    return jnp.concatenate([first, second], axis=axis)


def block_attend(queries, keys, values, mask, factor):
    scores = jnp.einsum("qhd,khd->qhk", queries, keys, preferred_element_type=jnp.float32) * factor
    if mask is None:
        peak = jnp.max(scores, axis=2)
        weights = jnp.exp(scores - peak[:, :, None])
    else:
        wide = mask[:, None, :]
        peak = jnp.max(jnp.where(wide, scores, NEG_BIG), axis=2)
        weights = jnp.where(wide, jnp.exp(jnp.where(wide, scores - peak[:, :, None], 0.0)), 0.0)
    total = jnp.sum(weights, axis=2)
    output = jnp.einsum(
        "qhk,khd->qhd", weights.astype(jnp.bfloat16), values, preferred_element_type=jnp.float32
    )
    return (peak, total, output)


def merge_parts(first, second):
    peak = jnp.maximum(first[0], second[0])
    weight_one = jnp.exp(first[0] - peak)
    weight_two = jnp.exp(second[0] - peak)
    total = first[1] * weight_one + second[1] * weight_two
    output = first[2] * weight_one[:, :, None, None] + second[2] * weight_two[:, :, None, None]
    return (peak, total, output)


def merge_both(first, second):
    return merge_parts(first[:3], second[:3]) + merge_parts(first[3:], second[3:])


def shards_split(
    activations,
    patch_index,
    modulation,
    qkv_weight,
    out_weight,
    stale_cache,
    id_cache,
    region_ids,
    id_counts,
):
    ksplit = lax.axis_size("ulys") // GROUPS
    nbits = ksplit.bit_length() - 1
    rank = lax.axis_index("ulys") % ksplit
    rows = activations[0]
    modul = modulation[0]
    lifted = rows.astype(jnp.float32)
    center = jnp.mean(lifted, axis=1, keepdims=True)
    spread = jnp.mean(jnp.square(lifted - center), axis=1, keepdims=True)
    normed = (lifted - center) * lax.rsqrt(spread + 1e-06)
    hidden = (normed * (1.0 + modul[1]) + modul[0]).astype(jnp.bfloat16)
    all_rows, all_regions = (
        lax.all_gather(hidden, "ulys", axis=0, tiled=True),
        lax.all_gather(region_ids[0].astype(jnp.bfloat16), "ulys", axis=0, tiled=True),
    )
    total_rows = all_rows.shape[0]
    weight = qkv_weight[0]
    block_dims = HD // ksplit
    pieces = jnp.dot(all_rows, weight, preferred_element_type=jnp.float32).astype(jnp.bfloat16)[
        :, None, :
    ]
    for level in range(nbits):
        partner = from_partner(as_sent(pieces), "ulys", level).astype(pieces.dtype)
        pieces = order_pair(pieces, partner, rank, level, 1)
    fields = (
        pieces.reshape(total_rows, ksplit, 3, HPD, block_dims)
        .transpose(2, 0, 3, 1, 4)
        .reshape(3, total_rows, HPD, HD)
    )
    queries = fields[0]
    stored = stale_cache[0, 0]
    span = stored.shape[0]
    old_keys = stored[:, 0].reshape(span, HPD, HD)
    old_values = stored[:, 1].reshape(span, HPD, HD)
    patch = patch_index[0]
    per_block = span // total_rows
    owner = patch // per_block
    offset = patch % per_block * total_rows
    keys = jnp.where(
        rank == owner, lax.dynamic_update_slice(old_keys, fields[1], (offset, 0, 0)), old_keys
    )
    values = jnp.where(
        rank == owner, lax.dynamic_update_slice(old_values, fields[2], (offset, 0, 0)), old_values
    )
    factor = HD ** (-0.5)
    query_block = min(512, total_rows)
    block_count = total_rows // query_block

    def attend_rows(query_rows):
        return block_attend(query_rows, keys, values, None, factor)

    peaks, totals, outputs = lax.map(
        attend_rows, queries.reshape(block_count, query_block, HPD, HD)
    )
    peaks = peaks.reshape(total_rows, HPD)
    totals = totals.reshape(total_rows, HPD)
    outputs = outputs.reshape(total_rows, HPD, ksplit, block_dims)
    guests = id_cache[0, 0]
    id_slots = guests.shape[1]
    guest_keys = guests[:, :, 0].reshape(SUBJ * id_slots, HPD, HD)
    guest_values = guests[:, :, 1].reshape(SUBJ * id_slots, HPD, HD)
    slot_index = jnp.arange(id_slots, dtype=jnp.int32) + rank * id_slots
    valid = slot_index[None, :] < id_counts[0][:, None]
    subject = jnp.arange(1, SUBJ + 1).astype(jnp.bfloat16)
    match = all_regions[:, None] == subject[None, :]
    mask = (match[:, :, None] & valid[None]).reshape(total_rows, SUBJ * id_slots)
    guest_peak, guest_total, guest_out = block_attend(
        queries, guest_keys, guest_values, mask, factor
    )
    guest_out = guest_out.reshape(total_rows, HPD, ksplit, block_dims)
    state = (peaks, totals, outputs, guest_peak, guest_total, guest_out)
    for level in range(nbits):
        partner = from_partner(state, "ulys", level)
        state = merge_both(state, partner)
    own_out = lax.dynamic_index_in_dim(state[2], rank, 2, keepdims=False)
    guest_final = lax.dynamic_index_in_dim(state[5], rank, 2, keepdims=False)
    own_final = own_out / state[1][:, :, None]
    guest_final = guest_final / jnp.maximum(state[4], 1.0)[:, :, None]
    mixed = (own_final + guest_final).astype(jnp.bfloat16).reshape(total_rows, HPD * block_dims)
    proj_weight = out_weight[0]
    added = lax.psum_scatter(
        jnp.dot(mixed, proj_weight, preferred_element_type=jnp.float32).astype(jnp.bfloat16),
        "ulys",
        scatter_dimension=0,
        tiled=True,
    ).astype(jnp.float32)
    result = (lifted + modul[2] * added).astype(jnp.bfloat16)
    return passed_along(result[None], "pipe", 1)


LANES = 128
MIB = 1 << 20
VMEM = pl.BlockSpec(memory_space=pltpu.VMEM)
SMEM = pl.BlockSpec(memory_space=pltpu.SMEM)
HBM = pl.BlockSpec(memory_space=pltpu.HBM)


def in_hbm(x):
    return pltpu.with_memory_space_constraint(x, pltpu.HBM)


def limit(mib):
    return pltpu.CompilerParams(vmem_limit_bytes=mib * MIB)


def modulate_kernel(rows_ref, modul_ref, region_ref, block_ref, rows, modul, regions, sems):
    tokens, width = rows.shape
    copies = [
        pltpu.make_async_copy(source, target, sems.at[i])
        for i, (source, target) in enumerate(((rows_ref, rows), (modul_ref, modul), (region_ref, regions)))
    ]
    for copy in copies:
        copy.start()
    for copy in copies:
        copy.wait()
    lifted = rows[...].astype(jnp.float32)
    center = jnp.mean(lifted, axis=1, keepdims=True)
    spread = jnp.mean(jnp.square(lifted - center), axis=1, keepdims=True)
    normed = (lifted - center) * lax.rsqrt(spread + 1e-06)
    hidden = normed * (1.0 + modul[1]) + modul[0]
    block_ref[:, :width] = hidden.astype(jnp.bfloat16)
    square = (tokens, tokens)
    diagonal = lax.broadcasted_iota(jnp.int32, square, 0) == lax.broadcasted_iota(jnp.int32, square, 1)
    region = jnp.broadcast_to(regions[...].astype(jnp.float32), square)
    column = jnp.sum(jnp.where(diagonal, region, 0.0), axis=1, keepdims=True)
    block_ref[:, width:] = jnp.broadcast_to(column, (tokens, LANES)).astype(jnp.bfloat16)


def modulate(rows, modul, region):
    tokens, width = rows.shape
    return pl.pallas_call(
        modulate_kernel,
        out_shape=jax.ShapeDtypeStruct((tokens, width + LANES), jnp.bfloat16),
        in_specs=[HBM] * 3,
        out_specs=VMEM,
        scratch_shapes=[
            pltpu.VMEM(rows.shape, rows.dtype),
            pltpu.VMEM(modul.shape, modul.dtype),
            pltpu.VMEM(region.shape, region.dtype),
            pltpu.SemaphoreType.DMA((3,)),
        ],
        compiler_params=limit(8),
        name="modulate",
    )(*map(in_hbm, (rows, modul, region)))


def stage_kernel(head, chunk, cache_ref, guest_ref, weight_ref, proj_ref, *refs):
    keys_ref, values_ref, weight_out, proj_out, held, wide, sems = refs
    span, slots = cache_ref.shape[0], guest_ref.shape[0]
    lanes = pl.ds(head * HD, HD)
    spans = [(at, chunk, cache_ref.at[pl.ds(at, chunk), :, lanes]) for at in range(0, span, chunk)]
    spans.append((span, slots, guest_ref.at[:, :, lanes]))
    copies = [
        pltpu.make_async_copy(source, held.at[pl.ds(at, count)], sems.at[i])
        for i, (at, count, source) in enumerate(spans)
    ]
    columns = pl.ds(head * weight_out.shape[1], weight_out.shape[1])
    copies.append(pltpu.make_async_copy(weight_ref.at[:, columns], weight_out, sems.at[len(spans)]))
    rows = pl.ds(head * HD, HD)
    copies.append(pltpu.make_async_copy(proj_ref.at[rows], proj_out, sems.at[len(spans) + 1]))
    for copy in copies:
        copy.start()
    pairs = held.reshape(2 * held.shape[0], HD)
    for (first, count, _), copy in zip(spans, copies):
        copy.wait()
        for at in range(first, first + count, LANES):
            step = min(LANES, first + count - at)
            slot = wide.at[at // LANES % wide.shape[0]]
            slot[pl.ds(0, 2 * step), :] = pairs[pl.ds(2 * at, 2 * step), :].astype(jnp.float32)
            keys_ref[:, pl.ds(at, step)] = slot[pl.ds(0, step, stride=2), :].T.astype(jnp.bfloat16)
            values_ref[pl.ds(at, step), :] = slot[pl.ds(1, step, stride=2), :].astype(jnp.bfloat16)
    for copy in copies[len(spans) :]:
        copy.wait()


def stage(head, cache, guests, weight, proj):
    span, slots = cache.shape[0], guests.shape[0]
    total = span + slots
    pieces = 4
    shapes = [(HD, total), (total, HD), (weight.shape[0], HPD * HD), (HD, proj.shape[1])]
    moved = 2 * (3 * total * HD + weight.size // 3 + proj.size // 3)
    return pl.pallas_call(
        functools.partial(stage_kernel, head, span // pieces),
        out_shape=[jax.ShapeDtypeStruct(shape, jnp.bfloat16) for shape in shapes],
        in_specs=[HBM] * 4,
        out_specs=[VMEM] * 4,
        scratch_shapes=[
            pltpu.VMEM((total, 2, HD), jnp.bfloat16),
            pltpu.VMEM((4, 2 * LANES, HD), jnp.float32),
            pltpu.SemaphoreType.DMA((pieces + 3,)),
        ],
        compiler_params=limit(8),
        cost_estimate=pl.CostEstimate(flops=0, bytes_accessed=moved, transcendentals=0),
        name="stage",
    )(*map(in_hbm, (cache, guests, weight, proj)))


def project_kernel(parts, place, patch_ref, *refs):
    blocks, weights, stored = refs[:parts], refs[parts : parts + 3], refs[parts + 3 : parts + 3 + 2 * HPD]
    query_ref, region_ref, *fresh_refs = refs[parts + 3 + 2 * HPD : -1]
    rows = refs[-1]
    tokens = blocks[0].shape[0]
    total = parts * tokens
    width = weights[0].shape[0]
    for r in range(parts):
        rows[pl.ds(r * tokens, tokens)] = blocks[r][...]
    region_ref[...] = rows[:, width:]
    fresh = pl.ds(pl.multiple_of((2 * patch_ref[0] + place) * total, total), total)
    for kind in range(3):
        field = jnp.dot(rows[:, :width], weights[kind][...], preferred_element_type=jnp.float32)
        field = field.astype(jnp.bfloat16)
        if kind == 0:
            query_ref[...] = field
            continue
        for h in range(HPD):
            part = field[:, h * HD : (h + 1) * HD]
            if kind == 1:
                fresh_refs[2 * h][:, fresh] = part.T
            else:
                fresh_refs[2 * h + 1][fresh, :] = part


def project(place, patch, blocks, weights, stored):
    parts = len(blocks)
    tokens, wide = blocks[0].shape
    total = parts * tokens
    out_shape = [
        jax.ShapeDtypeStruct((total, HPD * HD), jnp.bfloat16),
        jax.ShapeDtypeStruct((total, LANES), jnp.bfloat16),
    ]
    out_shape += [jax.ShapeDtypeStruct(array.shape, array.dtype) for array in stored]
    first = 1 + parts + 3
    return pl.pallas_call(
        functools.partial(project_kernel, parts, place),
        out_shape=out_shape,
        in_specs=[SMEM] + [VMEM] * (parts + 3 + 2 * HPD),
        out_specs=[VMEM] * len(out_shape),
        scratch_shapes=[pltpu.VMEM((total, wide), jnp.bfloat16)],
        input_output_aliases={first + i: 2 + i for i in range(2 * HPD)},
        compiler_params=limit(8),
        cost_estimate=pl.CostEstimate(
            flops=2 * total * (wide - LANES) * 3 * HPD * HD, bytes_accessed=8 * MIB, transcendentals=0
        ),
        name="project",
    )(patch, *blocks, *weights, *stored)


def attend_kernel(order, outputs, counts_ref, modul_ref, *refs):
    queries, regions, refs = refs[:2], refs[2:4], refs[4:]
    stored, refs = refs[: 2 * HPD], refs[2 * HPD :]
    projs, refs = refs[:HPD], refs[HPD:]
    outs, refs = refs[: len(outputs)], refs[len(outputs) :]
    scores, mixed = refs[:HPD], refs[HPD]
    total, span = scores[0].shape
    tokens = total // len(order)
    width = projs[0].shape[1]
    slots = stored[0].shape[1] - span
    each = slots // SUBJ

    def rows_of(arrays, columns):
        half = arrays[0].shape[0] // tokens
        return jnp.concatenate(
            [arrays[r // half][pl.ds(r % half * tokens, tokens), columns] for r in order], axis=0
        )

    lane = lax.broadcasted_iota(jnp.int32, (1, slots), 1)
    code = jnp.full((1, slots), -1.0, jnp.float32)
    for s in range(SUBJ):
        live = (lane >= s * each) & (lane < s * each + counts_ref[0, s])
        code = jnp.where(live, s + 1.0, code)
    match = code == rows_of(regions, pl.ds(0, LANES))[:, :1].astype(jnp.float32)
    factor = HD ** (-0.5) * math.log2(math.e)
    query = [rows_of(queries, pl.ds(h * HD, HD)) for h in range(HPD)]
    chunk = 256
    tops = [None] * HPD

    def score(h, at):
        found = jnp.dot(query[h], stored[2 * h][:, pl.ds(at, chunk)], preferred_element_type=jnp.float32)
        scores[h][:, pl.ds(at, chunk)] = found
        both = jnp.maximum(found[:, :LANES], found[:, LANES:])
        tops[h] = both if tops[h] is None else jnp.maximum(tops[h], both)

    for at in range(0, span, chunk):
        score(0, at)
    for h in range(HPD):
        keys, values = stored[2 * h], stored[2 * h + 1]
        peak = jnp.max(tops[h], axis=1, keepdims=True) * factor
        found = jnp.dot(query[h], keys[:, span:], preferred_element_type=jnp.float32) * factor
        sums = own = None
        for at in range(0, span, chunk):
            if h + 1 < HPD:
                score(h + 1, at)
            raised = jnp.exp2(scores[h][:, pl.ds(at, chunk)] * factor - peak)
            both = raised[:, :LANES] + raised[:, LANES:]
            product = jnp.dot(
                raised.astype(jnp.bfloat16), values[pl.ds(at, chunk), :], preferred_element_type=jnp.float32
            )
            sums = both if sums is None else sums + both
            own = product if own is None else own + product
        own = own / jnp.sum(sums, axis=1, keepdims=True)
        peak = jnp.max(jnp.where(match, found, NEG_BIG), axis=1, keepdims=True)
        raised = jnp.where(match, jnp.exp2(jnp.where(match, found - peak, 0.0)), 0.0)
        guest = jnp.dot(raised.astype(jnp.bfloat16), values[span:, :], preferred_element_type=jnp.float32)
        guest = guest / jnp.maximum(jnp.sum(raised, axis=1, keepdims=True), 1.0)
        mixed[:, pl.ds(h * HD, HD)] = (own + guest).astype(jnp.bfloat16)
    for at in range(0, width, 512):
        columns = pl.ds(at, 512)
        proj = jnp.concatenate([share[:, columns] for share in projs], axis=0)
        part = jnp.dot(mixed[...], proj, preferred_element_type=jnp.float32) * modul_ref[2, :, columns]
        first = 0
        for out, count in zip(outs, outputs):
            terms = part[first : first + count * tokens]
            out[pl.ds(0, terms.shape[0]), columns] = terms.astype(out.dtype)
            first += count * tokens


def attend(order, outputs, tokens, span, counts, modul, queries, regions, stored, projs):
    total = len(order) * tokens
    width = projs[0].shape[1]
    return pl.pallas_call(
        functools.partial(attend_kernel, order, [count for count, _ in outputs]),
        out_shape=[jax.ShapeDtypeStruct((count * tokens, width), kind) for count, kind in outputs],
        in_specs=[SMEM] + [VMEM] * (5 + 3 * HPD),
        out_specs=[VMEM] * len(outputs),
        scratch_shapes=[pltpu.VMEM((total, span), jnp.float32)] * HPD
        + [pltpu.VMEM((total, HPD * HD), jnp.bfloat16)],
        compiler_params=limit(16),
        cost_estimate=pl.CostEstimate(
            flops=2 * total * HPD * HD * (width + 2 * span),
            bytes_accessed=16 * MIB,
            transcendentals=HPD * total * span,
        ),
        name="attend",
    )(counts, modul, *queries, *regions, *stored, *projs)


def add_kernel(kept_ref, *refs):
    total = kept_ref[...]
    for came_ref in refs[:-1]:
        total = total + came_ref[...].astype(jnp.float32)
    refs[-1][...] = total.astype(jnp.bfloat16)


def add_terms(kept, *came):
    return pl.pallas_call(
        add_kernel,
        out_shape=jax.ShapeDtypeStruct(kept.shape, jnp.bfloat16),
        in_specs=[VMEM] * (1 + len(came)),
        out_specs=VMEM,
        compiler_params=limit(4),
        name="add_terms",
    )(kept, *came)


def shards_whole(
    activations,
    patch_index,
    modulation,
    qkv_weight,
    out_weight,
    stale_cache,
    id_cache,
    region_ids,
    id_counts,
):
    pipes, group = lax.axis_size("pipe"), lax.axis_size("ulys")

    def beside(x, apart):
        return lax.ppermute(x, "ulys", [(i, i ^ apart) for i in range(group)])

    def onward(x, apart):
        pairs = [
            (p * group + i, (p + 1) % pipes * group + (i ^ apart))
            for p in range(pipes)
            for i in range(group)
        ]
        return lax.ppermute(x, ("pipe", "ulys"), pairs)

    hold = lax.optimization_barrier
    rows = activations[0]
    tokens = rows.shape[0]
    modul = modulation.transpose(1, 0, 2)
    stored = stale_cache[0, 0]
    guests = id_cache[0, 0]
    guests = guests.reshape(SUBJ * guests.shape[1], 2, HPD * HD)
    staged = functools.partial(stage, cache=stored, guests=guests, weight=qkv_weight[0], proj=out_weight[0])
    b0 = modulate(rows, modul, region_ids)
    b4, b1, b3, b2 = (beside(b0, r) for r in (4, 1, 3, 2))
    heads = [staged(h) for h in range(HPD)]
    b4, *early = hold((b4, *heads[0], *heads[1]))
    heads[0], heads[1] = early[: len(heads[0])], early[len(heads[0]) :]
    b7, b5, b6 = beside(b4, 3), beside(b4, 1), beside(b4, 2)
    weights, fields = [head[2] for head in heads], [array for head in heads for array in head[:2]]
    query_near, region_near, *fields = project(0, patch_index, (b0, b1, b2, b3), weights, fields)
    query_far, region_far, *fields = project(1, patch_index, (b4, b5, b6, b7), weights, fields)
    attended = functools.partial(
        attend,
        tokens=tokens,
        span=stored.shape[0],
        counts=id_counts,
        modul=modul,
        regions=(region_near, region_far),
        stored=fields,
        projs=[head[3] for head in heads],
    )
    narrow, wide = (1, jnp.bfloat16), (1, jnp.float32)
    t4, t7, t5, t6 = attended((4, 7, 5, 6), [wide] + [narrow] * 3, queries=(query_near, query_far))
    t4, t7, t5, t6, query_near = hold((t4, t7, t5, t6, query_near))
    t3, t1, t2, t0 = attended((3, 1, 2, 0), [narrow] * 4, queries=(query_near, query_far))
    c7, c5, c6 = beside(t7, 3), beside(t5, 1), beside(t6, 2)
    rows, t3, t1, t2, t0 = hold((rows, t3, t1, t2, t0))
    before = onward(rows, 0)
    c3, c1, c2 = onward(t3, 3), onward(t1, 1), onward(t2, 2)
    s4 = add_terms(t4, c7, c5, c6)
    s4, t0 = hold((s4, t0))
    parts = before, c3, c1, c2, onward(s4, 4), onward(t0, 0)
    return sum(part.astype(jnp.float32) for part in parts).astype(jnp.bfloat16)[None]


def shards(*arrays):
    return (shards_whole if lax.axis_size("ulys") == GROUPS else shards_split)(*arrays)


def solution(mesh):
    placed = (
        P("pipe", "ulys", None),
        P("pipe"),
        P("pipe", None, None),
        P("pipe", None, "ulys"),
        P("pipe", "ulys", None),
        P("pipe", "ulys", None, None, None),
        P("pipe", "ulys", None, None, None, None),
        P("pipe", "ulys"),
        P("pipe", None),
    )
    return jax.shard_map(
        shards, mesh=mesh, in_specs=placed, out_specs=P("pipe", "ulys", None), check_vma=False
    )
```

```python
import functools
import math

import jax
import jax.numpy as jnp
from jax import lax
from jax.experimental import pallas as pl
from jax.experimental.pallas import tpu as pltpu
from jax.sharding import PartitionSpec as P

HD = 128
HPD = 3
GROUPS = 8
SUBJ = 6


NEG_BIG = -1e30


def as_sent(x):
    return jax.tree.map(lambda a: a.astype(jnp.bfloat16) if a.dtype == jnp.float32 else a, x)


def from_partner(x, axis, apart):
    return lax.ppermute(x, axis, [(i, i ^ 1 << apart) for i in range(lax.axis_size(axis))])


def passed_along(x, axis, by):
    size = lax.axis_size(axis)
    return lax.ppermute(x, axis, [(i, (i + by) % size) for i in range(size)])


def order_pair(mine, other, rank, level, axis):
    upper = rank // 2**level % 2
    first = jnp.where(upper == 1, other, mine)
    second = jnp.where(upper == 1, mine, other)
    return jnp.concatenate([first, second], axis=axis)


def block_attend(queries, keys, values, mask, factor):
    scores = jnp.einsum("qhd,khd->qhk", queries, keys, preferred_element_type=jnp.float32) * factor
    if mask is None:
        peak = jnp.max(scores, axis=2)
        weights = jnp.exp(scores - peak[:, :, None])
    else:
        wide = mask[:, None, :]
        peak = jnp.max(jnp.where(wide, scores, NEG_BIG), axis=2)
        weights = jnp.where(wide, jnp.exp(jnp.where(wide, scores - peak[:, :, None], 0.0)), 0.0)
    total = jnp.sum(weights, axis=2)
    output = jnp.einsum(
        "qhk,khd->qhd", weights.astype(jnp.bfloat16), values, preferred_element_type=jnp.float32
    )
    return (peak, total, output)


def merge_parts(first, second):
    peak = jnp.maximum(first[0], second[0])
    weight_one = jnp.exp(first[0] - peak)
    weight_two = jnp.exp(second[0] - peak)
    total = first[1] * weight_one + second[1] * weight_two
    output = first[2] * weight_one[:, :, None, None] + second[2] * weight_two[:, :, None, None]
    return (peak, total, output)


def merge_both(first, second):
    return merge_parts(first[:3], second[:3]) + merge_parts(first[3:], second[3:])


def shards_split(
    activations,
    patch_index,
    modulation,
    qkv_weight,
    out_weight,
    stale_cache,
    id_cache,
    region_ids,
    id_counts,
):
    ksplit = lax.axis_size("ulys") // GROUPS
    nbits = ksplit.bit_length() - 1
    rank = lax.axis_index("ulys") % ksplit
    rows = activations[0]
    modul = modulation[0]
    lifted = rows.astype(jnp.float32)
    center = jnp.mean(lifted, axis=1, keepdims=True)
    spread = jnp.mean(jnp.square(lifted - center), axis=1, keepdims=True)
    normed = (lifted - center) * lax.rsqrt(spread + 1e-06)
    hidden = (normed * (1.0 + modul[1]) + modul[0]).astype(jnp.bfloat16)
    all_rows, all_regions = (
        lax.all_gather(hidden, "ulys", axis=0, tiled=True),
        lax.all_gather(region_ids[0].astype(jnp.bfloat16), "ulys", axis=0, tiled=True),
    )
    total_rows = all_rows.shape[0]
    weight = qkv_weight[0]
    block_dims = HD // ksplit
    pieces = jnp.dot(all_rows, weight, preferred_element_type=jnp.float32).astype(jnp.bfloat16)[
        :, None, :
    ]
    for level in range(nbits):
        partner = from_partner(as_sent(pieces), "ulys", level).astype(pieces.dtype)
        pieces = order_pair(pieces, partner, rank, level, 1)
    fields = (
        pieces.reshape(total_rows, ksplit, 3, HPD, block_dims)
        .transpose(2, 0, 3, 1, 4)
        .reshape(3, total_rows, HPD, HD)
    )
    queries = fields[0]
    stored = stale_cache[0, 0]
    span = stored.shape[0]
    old_keys = stored[:, 0].reshape(span, HPD, HD)
    old_values = stored[:, 1].reshape(span, HPD, HD)
    patch = patch_index[0]
    per_block = span // total_rows
    owner = patch // per_block
    offset = patch % per_block * total_rows
    keys = jnp.where(
        rank == owner, lax.dynamic_update_slice(old_keys, fields[1], (offset, 0, 0)), old_keys
    )
    values = jnp.where(
        rank == owner, lax.dynamic_update_slice(old_values, fields[2], (offset, 0, 0)), old_values
    )
    factor = HD ** (-0.5)
    query_block = min(512, total_rows)
    block_count = total_rows // query_block

    def attend_rows(query_rows):
        return block_attend(query_rows, keys, values, None, factor)

    peaks, totals, outputs = lax.map(
        attend_rows, queries.reshape(block_count, query_block, HPD, HD)
    )
    peaks = peaks.reshape(total_rows, HPD)
    totals = totals.reshape(total_rows, HPD)
    outputs = outputs.reshape(total_rows, HPD, ksplit, block_dims)
    guests = id_cache[0, 0]
    id_slots = guests.shape[1]
    guest_keys = guests[:, :, 0].reshape(SUBJ * id_slots, HPD, HD)
    guest_values = guests[:, :, 1].reshape(SUBJ * id_slots, HPD, HD)
    slot_index = jnp.arange(id_slots, dtype=jnp.int32) + rank * id_slots
    valid = slot_index[None, :] < id_counts[0][:, None]
    subject = jnp.arange(1, SUBJ + 1).astype(jnp.bfloat16)
    match = all_regions[:, None] == subject[None, :]
    mask = (match[:, :, None] & valid[None]).reshape(total_rows, SUBJ * id_slots)
    guest_peak, guest_total, guest_out = block_attend(
        queries, guest_keys, guest_values, mask, factor
    )
    guest_out = guest_out.reshape(total_rows, HPD, ksplit, block_dims)
    state = (peaks, totals, outputs, guest_peak, guest_total, guest_out)
    for level in range(nbits):
        partner = from_partner(state, "ulys", level)
        state = merge_both(state, partner)
    own_out = lax.dynamic_index_in_dim(state[2], rank, 2, keepdims=False)
    guest_final = lax.dynamic_index_in_dim(state[5], rank, 2, keepdims=False)
    own_final = own_out / state[1][:, :, None]
    guest_final = guest_final / jnp.maximum(state[4], 1.0)[:, :, None]
    mixed = (own_final + guest_final).astype(jnp.bfloat16).reshape(total_rows, HPD * block_dims)
    proj_weight = out_weight[0]
    added = lax.psum_scatter(
        jnp.dot(mixed, proj_weight, preferred_element_type=jnp.float32).astype(jnp.bfloat16),
        "ulys",
        scatter_dimension=0,
        tiled=True,
    ).astype(jnp.float32)
    result = (lifted + modul[2] * added).astype(jnp.bfloat16)
    return passed_along(result[None], "pipe", 1)


LANES = 128
MIB = 1 << 20
VMEM = pl.BlockSpec(memory_space=pltpu.VMEM)
SMEM = pl.BlockSpec(memory_space=pltpu.SMEM)
HBM = pl.BlockSpec(memory_space=pltpu.HBM)


def in_hbm(x):
    return pltpu.with_memory_space_constraint(x, pltpu.HBM)


def limit(mib):
    return pltpu.CompilerParams(vmem_limit_bytes=mib * MIB)


def modulate_kernel(rows_ref, modul_ref, region_ref, block_ref, rows, modul, regions, sems):
    tokens, width = rows.shape
    copies = [
        pltpu.make_async_copy(source, target, sems.at[i])
        for i, (source, target) in enumerate(((rows_ref, rows), (modul_ref, modul), (region_ref, regions)))
    ]
    for copy in copies:
        copy.start()
    for copy in copies:
        copy.wait()
    lifted = rows[...].astype(jnp.float32)
    center = jnp.mean(lifted, axis=1, keepdims=True)
    spread = jnp.mean(jnp.square(lifted - center), axis=1, keepdims=True)
    normed = (lifted - center) * lax.rsqrt(spread + 1e-06)
    hidden = normed * (1.0 + modul[1]) + modul[0]
    block_ref[:, :width] = hidden.astype(jnp.bfloat16)
    square = (tokens, tokens)
    diagonal = lax.broadcasted_iota(jnp.int32, square, 0) == lax.broadcasted_iota(jnp.int32, square, 1)
    region = jnp.broadcast_to(regions[...].astype(jnp.float32), square)
    column = jnp.sum(jnp.where(diagonal, region, 0.0), axis=1, keepdims=True)
    block_ref[:, width:] = jnp.broadcast_to(column, (tokens, LANES)).astype(jnp.bfloat16)


def modulate(rows, modul, region):
    tokens, width = rows.shape
    return pl.pallas_call(
        modulate_kernel,
        out_shape=jax.ShapeDtypeStruct((tokens, width + LANES), jnp.bfloat16),
        in_specs=[HBM] * 3,
        out_specs=VMEM,
        scratch_shapes=[
            pltpu.VMEM(rows.shape, rows.dtype),
            pltpu.VMEM(modul.shape, modul.dtype),
            pltpu.VMEM(region.shape, region.dtype),
            pltpu.SemaphoreType.DMA((3,)),
        ],
        compiler_params=limit(8),
        name="modulate",
    )(*map(in_hbm, (rows, modul, region)))


def stage_kernel(head, chunk, cache_ref, guest_ref, weight_ref, proj_ref, *refs):
    keys_ref, values_ref, weight_out, proj_out, held, wide, sems = refs
    span, slots = cache_ref.shape[0], guest_ref.shape[0]
    lanes = pl.ds(head * HD, HD)
    spans = [(at, chunk, cache_ref.at[pl.ds(at, chunk), :, lanes]) for at in range(0, span, chunk)]
    spans.append((span, slots, guest_ref.at[:, :, lanes]))
    copies = [
        pltpu.make_async_copy(source, held.at[pl.ds(at, count)], sems.at[i])
        for i, (at, count, source) in enumerate(spans)
    ]
    columns = pl.ds(head * weight_out.shape[1], weight_out.shape[1])
    copies.append(pltpu.make_async_copy(weight_ref.at[:, columns], weight_out, sems.at[len(spans)]))
    rows = pl.ds(head * HD, HD)
    copies.append(pltpu.make_async_copy(proj_ref.at[rows], proj_out, sems.at[len(spans) + 1]))
    for copy in copies:
        copy.start()
    pairs = held.reshape(2 * held.shape[0], HD)
    for (first, count, _), copy in zip(spans, copies):
        copy.wait()
        for at in range(first, first + count, LANES):
            step = min(LANES, first + count - at)
            slot = wide.at[at // LANES % wide.shape[0]]
            slot[pl.ds(0, 2 * step), :] = pairs[pl.ds(2 * at, 2 * step), :].astype(jnp.float32)
            keys_ref[:, pl.ds(at, step)] = slot[pl.ds(0, step, stride=2), :].T.astype(jnp.bfloat16)
            values_ref[pl.ds(at, step), :] = slot[pl.ds(1, step, stride=2), :].astype(jnp.bfloat16)
    for copy in copies[len(spans) :]:
        copy.wait()


def stage(head, cache, guests, weight, proj):
    span, slots = cache.shape[0], guests.shape[0]
    total = span + slots
    pieces = 4
    shapes = [(HD, total), (total, HD), (weight.shape[0], HPD * HD), (HD, proj.shape[1])]
    moved = 2 * (3 * total * HD + weight.size // 3 + proj.size // 3)
    return pl.pallas_call(
        functools.partial(stage_kernel, head, span // pieces),
        out_shape=[jax.ShapeDtypeStruct(shape, jnp.bfloat16) for shape in shapes],
        in_specs=[HBM] * 4,
        out_specs=[VMEM] * 4,
        scratch_shapes=[
            pltpu.VMEM((total, 2, HD), jnp.bfloat16),
            pltpu.VMEM((4, 2 * LANES, HD), jnp.float32),
            pltpu.SemaphoreType.DMA((pieces + 3,)),
        ],
        compiler_params=limit(8),
        cost_estimate=pl.CostEstimate(flops=0, bytes_accessed=moved, transcendentals=0),
        name="stage",
    )(*map(in_hbm, (cache, guests, weight, proj)))


def project_kernel(parts, place, patch_ref, *refs):
    blocks, weights, stored = refs[:parts], refs[parts : parts + 3], refs[parts + 3 : parts + 3 + 2 * HPD]
    query_ref, region_ref, *fresh_refs = refs[parts + 3 + 2 * HPD : -1]
    rows = refs[-1]
    tokens = blocks[0].shape[0]
    total = parts * tokens
    width = weights[0].shape[0]
    for r in range(parts):
        rows[pl.ds(r * tokens, tokens)] = blocks[r][...]
    region_ref[...] = rows[:, width:]
    fresh = pl.ds(pl.multiple_of((2 * patch_ref[0] + place) * total, total), total)
    for kind in range(3):
        field = jnp.dot(rows[:, :width], weights[kind][...], preferred_element_type=jnp.float32)
        field = field.astype(jnp.bfloat16)
        if kind == 0:
            query_ref[...] = field
            continue
        for h in range(HPD):
            part = field[:, h * HD : (h + 1) * HD]
            if kind == 1:
                fresh_refs[2 * h][:, fresh] = part.T
            else:
                fresh_refs[2 * h + 1][fresh, :] = part


def project(place, patch, blocks, weights, stored):
    parts = len(blocks)
    tokens, wide = blocks[0].shape
    total = parts * tokens
    out_shape = [
        jax.ShapeDtypeStruct((total, HPD * HD), jnp.bfloat16),
        jax.ShapeDtypeStruct((total, LANES), jnp.bfloat16),
    ]
    out_shape += [jax.ShapeDtypeStruct(array.shape, array.dtype) for array in stored]
    first = 1 + parts + 3
    return pl.pallas_call(
        functools.partial(project_kernel, parts, place),
        out_shape=out_shape,
        in_specs=[SMEM] + [VMEM] * (parts + 3 + 2 * HPD),
        out_specs=[VMEM] * len(out_shape),
        scratch_shapes=[pltpu.VMEM((total, wide), jnp.bfloat16)],
        input_output_aliases={first + i: 2 + i for i in range(2 * HPD)},
        compiler_params=limit(8),
        cost_estimate=pl.CostEstimate(
            flops=2 * total * (wide - LANES) * 3 * HPD * HD, bytes_accessed=8 * MIB, transcendentals=0
        ),
        name="project",
    )(patch, *blocks, *weights, *stored)


def attend_kernel(order, outputs, counts_ref, modul_ref, *refs):
    queries, regions, refs = refs[:2], refs[2:4], refs[4:]
    stored, refs = refs[: 2 * HPD], refs[2 * HPD :]
    projs, refs = refs[:HPD], refs[HPD:]
    outs, refs = refs[: len(outputs)], refs[len(outputs) :]
    scores, mixed = refs[:HPD], refs[HPD]
    total, span = scores[0].shape
    tokens = total // len(order)
    width = projs[0].shape[1]
    slots = stored[0].shape[1] - span
    each = slots // SUBJ

    def rows_of(arrays, columns):
        half = arrays[0].shape[0] // tokens
        return jnp.concatenate(
            [arrays[r // half][pl.ds(r % half * tokens, tokens), columns] for r in order], axis=0
        )

    lane = lax.broadcasted_iota(jnp.int32, (1, slots), 1)
    code = jnp.full((1, slots), -1.0, jnp.float32)
    for s in range(SUBJ):
        live = (lane >= s * each) & (lane < s * each + counts_ref[0, s])
        code = jnp.where(live, s + 1.0, code)
    match = code == rows_of(regions, pl.ds(0, LANES))[:, :1].astype(jnp.float32)
    factor = HD ** (-0.5) * math.log2(math.e)
    query = [rows_of(queries, pl.ds(h * HD, HD)) for h in range(HPD)]
    chunk = 512
    tops = [None] * HPD

    def fold(join, found, whole):
        parts = [found[:, i : i + LANES] for i in range(0, found.shape[1], LANES)]
        return functools.reduce(join, parts if whole is None else [whole, *parts])

    def score(h, at):
        found = jnp.dot(query[h], stored[2 * h][:, pl.ds(at, chunk)], preferred_element_type=jnp.float32)
        scores[h][:, pl.ds(at, chunk)] = found
        tops[h] = fold(jnp.maximum, found, tops[h])

    for at in range(0, span, chunk):
        score(0, at)
    for h in range(HPD):
        keys, values = stored[2 * h], stored[2 * h + 1]
        peak = jnp.max(tops[h], axis=1, keepdims=True) * factor
        found = jnp.dot(query[h], keys[:, span:], preferred_element_type=jnp.float32) * factor
        sums = own = None
        for at in range(0, span, chunk):
            if h + 1 < HPD:
                score(h + 1, at)
            raised = jnp.exp2(scores[h][:, pl.ds(at, chunk)] * factor - peak)
            sums = fold(jnp.add, raised, sums)
            product = jnp.dot(
                raised.astype(jnp.bfloat16), values[pl.ds(at, chunk), :], preferred_element_type=jnp.float32
            )
            own = product if own is None else own + product
        own = own / jnp.sum(sums, axis=1, keepdims=True)
        peak = jnp.max(jnp.where(match, found, NEG_BIG), axis=1, keepdims=True)
        raised = jnp.where(match, jnp.exp2(jnp.where(match, found - peak, 0.0)), 0.0)
        guest = jnp.dot(raised.astype(jnp.bfloat16), values[span:, :], preferred_element_type=jnp.float32)
        guest = guest / jnp.maximum(jnp.sum(raised, axis=1, keepdims=True), 1.0)
        mixed[:, pl.ds(h * HD, HD)] = (own + guest).astype(jnp.bfloat16)
    for at in range(0, width, 512):
        columns = pl.ds(at, 512)
        proj = jnp.concatenate([share[:, columns] for share in projs], axis=0)
        part = jnp.dot(mixed[...], proj, preferred_element_type=jnp.float32) * modul_ref[2, :, columns]
        first = 0
        for out, count in zip(outs, outputs):
            terms = part[first : first + count * tokens]
            out[pl.ds(0, terms.shape[0]), columns] = terms.astype(out.dtype)
            first += count * tokens


def attend(order, outputs, tokens, span, counts, modul, queries, regions, stored, projs):
    total = len(order) * tokens
    width = projs[0].shape[1]
    return pl.pallas_call(
        functools.partial(attend_kernel, order, [count for count, _ in outputs]),
        out_shape=[jax.ShapeDtypeStruct((count * tokens, width), kind) for count, kind in outputs],
        in_specs=[SMEM] + [VMEM] * (5 + 3 * HPD),
        out_specs=[VMEM] * len(outputs),
        scratch_shapes=[pltpu.VMEM((total, span), jnp.float32)] * HPD
        + [pltpu.VMEM((total, HPD * HD), jnp.bfloat16)],
        compiler_params=limit(16),
        cost_estimate=pl.CostEstimate(
            flops=2 * total * HPD * HD * (width + 2 * span),
            bytes_accessed=16 * MIB,
            transcendentals=HPD * total * span,
        ),
        name="attend",
    )(counts, modul, *queries, *regions, *stored, *projs)


def add_kernel(kept_ref, *refs):
    total = kept_ref[...]
    for came_ref in refs[:-1]:
        total = total + came_ref[...].astype(jnp.float32)
    refs[-1][...] = total.astype(jnp.bfloat16)


def add_terms(kept, *came):
    return pl.pallas_call(
        add_kernel,
        out_shape=jax.ShapeDtypeStruct(kept.shape, jnp.bfloat16),
        in_specs=[VMEM] * (1 + len(came)),
        out_specs=VMEM,
        compiler_params=limit(4),
        name="add_terms",
    )(kept, *came)


def shards_whole(
    activations,
    patch_index,
    modulation,
    qkv_weight,
    out_weight,
    stale_cache,
    id_cache,
    region_ids,
    id_counts,
):
    pipes, group = lax.axis_size("pipe"), lax.axis_size("ulys")

    def beside(x, apart):
        return lax.ppermute(x, "ulys", [(i, i ^ apart) for i in range(group)])

    def onward(x, apart):
        pairs = [
            (p * group + i, (p + 1) % pipes * group + (i ^ apart))
            for p in range(pipes)
            for i in range(group)
        ]
        return lax.ppermute(x, ("pipe", "ulys"), pairs)

    hold = lax.optimization_barrier
    rows = activations[0]
    tokens = rows.shape[0]
    modul = modulation.transpose(1, 0, 2)
    stored = stale_cache[0, 0]
    guests = id_cache[0, 0]
    guests = guests.reshape(SUBJ * guests.shape[1], 2, HPD * HD)
    staged = functools.partial(stage, cache=stored, guests=guests, weight=qkv_weight[0], proj=out_weight[0])
    b0 = modulate(rows, modul, region_ids)
    b4, b1, b3, b2 = (beside(b0, r) for r in (4, 1, 3, 2))
    heads = [staged(h) for h in range(HPD)]
    b4, *early = hold((b4, *heads[0], *heads[1]))
    heads[0], heads[1] = early[: len(heads[0])], early[len(heads[0]) :]
    b7, b5, b6 = beside(b4, 3), beside(b4, 1), beside(b4, 2)
    weights, fields = [head[2] for head in heads], [array for head in heads for array in head[:2]]
    query_near, region_near, *fields = project(0, patch_index, (b0, b1, b2, b3), weights, fields)
    query_far, region_far, *fields = project(1, patch_index, (b4, b5, b6, b7), weights, fields)
    attended = functools.partial(
        attend,
        tokens=tokens,
        span=stored.shape[0],
        counts=id_counts,
        modul=modul,
        regions=(region_near, region_far),
        stored=fields,
        projs=[head[3] for head in heads],
    )
    narrow, wide = (1, jnp.bfloat16), (1, jnp.float32)
    t4, t7, t5, t6 = attended((4, 7, 5, 6), [wide] + [narrow] * 3, queries=(query_near, query_far))
    t4, t7, t5, t6, query_near = hold((t4, t7, t5, t6, query_near))
    t3, t1, t2, t0 = attended((3, 1, 2, 0), [narrow] * 4, queries=(query_near, query_far))
    c7, c5, c6 = beside(t7, 3), beside(t5, 1), beside(t6, 2)
    rows, t3, t1, t2, t0 = hold((rows, t3, t1, t2, t0))
    before = onward(rows, 0)
    c3, c1, c2 = onward(t3, 3), onward(t1, 1), onward(t2, 2)
    s4 = add_terms(t4, c7, c5, c6)
    s4, t0 = hold((s4, t0))
    parts = before, c3, c1, c2, onward(s4, 4), onward(t0, 0)
    return sum(part.astype(jnp.float32) for part in parts).astype(jnp.bfloat16)[None]


def shards(*arrays):
    return (shards_whole if lax.axis_size("ulys") == GROUPS else shards_split)(*arrays)


def solution(mesh):
    placed = (
        P("pipe", "ulys", None),
        P("pipe"),
        P("pipe", None, None),
        P("pipe", None, "ulys"),
        P("pipe", "ulys", None),
        P("pipe", "ulys", None, None, None),
        P("pipe", "ulys", None, None, None, None),
        P("pipe", "ulys"),
        P("pipe", None),
    )
    return jax.shard_map(
        shards, mesh=mesh, in_specs=placed, out_specs=P("pipe", "ulys", None), check_vma=False
    )
```

```python
import functools
import math

import jax
import jax.numpy as jnp
from jax import lax
from jax.experimental import pallas as pl
from jax.experimental.pallas import tpu as pltpu
from jax.sharding import PartitionSpec as P

HD = 128
HPD = 3
GROUPS = 8
SUBJ = 6


NEG_BIG = -1e30


def as_sent(x):
    return jax.tree.map(lambda a: a.astype(jnp.bfloat16) if a.dtype == jnp.float32 else a, x)


def from_partner(x, axis, apart):
    return lax.ppermute(x, axis, [(i, i ^ 1 << apart) for i in range(lax.axis_size(axis))])


def passed_along(x, axis, by):
    size = lax.axis_size(axis)
    return lax.ppermute(x, axis, [(i, (i + by) % size) for i in range(size)])


def order_pair(mine, other, rank, level, axis):
    upper = rank // 2**level % 2
    first = jnp.where(upper == 1, other, mine)
    second = jnp.where(upper == 1, mine, other)
    return jnp.concatenate([first, second], axis=axis)


def block_attend(queries, keys, values, mask, factor):
    scores = jnp.einsum("qhd,khd->qhk", queries, keys, preferred_element_type=jnp.float32) * factor
    if mask is None:
        peak = jnp.max(scores, axis=2)
        weights = jnp.exp(scores - peak[:, :, None])
    else:
        wide = mask[:, None, :]
        peak = jnp.max(jnp.where(wide, scores, NEG_BIG), axis=2)
        weights = jnp.where(wide, jnp.exp(jnp.where(wide, scores - peak[:, :, None], 0.0)), 0.0)
    total = jnp.sum(weights, axis=2)
    output = jnp.einsum(
        "qhk,khd->qhd", weights.astype(jnp.bfloat16), values, preferred_element_type=jnp.float32
    )
    return (peak, total, output)


def merge_parts(first, second):
    peak = jnp.maximum(first[0], second[0])
    weight_one = jnp.exp(first[0] - peak)
    weight_two = jnp.exp(second[0] - peak)
    total = first[1] * weight_one + second[1] * weight_two
    output = first[2] * weight_one[:, :, None, None] + second[2] * weight_two[:, :, None, None]
    return (peak, total, output)


def merge_both(first, second):
    return merge_parts(first[:3], second[:3]) + merge_parts(first[3:], second[3:])


def shards_split(
    activations,
    patch_index,
    modulation,
    qkv_weight,
    out_weight,
    stale_cache,
    id_cache,
    region_ids,
    id_counts,
):
    ksplit = lax.axis_size("ulys") // GROUPS
    nbits = ksplit.bit_length() - 1
    rank = lax.axis_index("ulys") % ksplit
    rows = activations[0]
    modul = modulation[0]
    lifted = rows.astype(jnp.float32)
    center = jnp.mean(lifted, axis=1, keepdims=True)
    spread = jnp.mean(jnp.square(lifted - center), axis=1, keepdims=True)
    normed = (lifted - center) * lax.rsqrt(spread + 1e-06)
    hidden = (normed * (1.0 + modul[1]) + modul[0]).astype(jnp.bfloat16)
    all_rows, all_regions = (
        lax.all_gather(hidden, "ulys", axis=0, tiled=True),
        lax.all_gather(region_ids[0].astype(jnp.bfloat16), "ulys", axis=0, tiled=True),
    )
    total_rows = all_rows.shape[0]
    weight = qkv_weight[0]
    block_dims = HD // ksplit
    pieces = jnp.dot(all_rows, weight, preferred_element_type=jnp.float32).astype(jnp.bfloat16)[
        :, None, :
    ]
    for level in range(nbits):
        partner = from_partner(as_sent(pieces), "ulys", level).astype(pieces.dtype)
        pieces = order_pair(pieces, partner, rank, level, 1)
    fields = (
        pieces.reshape(total_rows, ksplit, 3, HPD, block_dims)
        .transpose(2, 0, 3, 1, 4)
        .reshape(3, total_rows, HPD, HD)
    )
    queries = fields[0]
    stored = stale_cache[0, 0]
    span = stored.shape[0]
    old_keys = stored[:, 0].reshape(span, HPD, HD)
    old_values = stored[:, 1].reshape(span, HPD, HD)
    patch = patch_index[0]
    per_block = span // total_rows
    owner = patch // per_block
    offset = patch % per_block * total_rows
    keys = jnp.where(
        rank == owner, lax.dynamic_update_slice(old_keys, fields[1], (offset, 0, 0)), old_keys
    )
    values = jnp.where(
        rank == owner, lax.dynamic_update_slice(old_values, fields[2], (offset, 0, 0)), old_values
    )
    factor = HD ** (-0.5)
    query_block = min(512, total_rows)
    block_count = total_rows // query_block

    def attend_rows(query_rows):
        return block_attend(query_rows, keys, values, None, factor)

    peaks, totals, outputs = lax.map(
        attend_rows, queries.reshape(block_count, query_block, HPD, HD)
    )
    peaks = peaks.reshape(total_rows, HPD)
    totals = totals.reshape(total_rows, HPD)
    outputs = outputs.reshape(total_rows, HPD, ksplit, block_dims)
    guests = id_cache[0, 0]
    id_slots = guests.shape[1]
    guest_keys = guests[:, :, 0].reshape(SUBJ * id_slots, HPD, HD)
    guest_values = guests[:, :, 1].reshape(SUBJ * id_slots, HPD, HD)
    slot_index = jnp.arange(id_slots, dtype=jnp.int32) + rank * id_slots
    valid = slot_index[None, :] < id_counts[0][:, None]
    subject = jnp.arange(1, SUBJ + 1).astype(jnp.bfloat16)
    match = all_regions[:, None] == subject[None, :]
    mask = (match[:, :, None] & valid[None]).reshape(total_rows, SUBJ * id_slots)
    guest_peak, guest_total, guest_out = block_attend(
        queries, guest_keys, guest_values, mask, factor
    )
    guest_out = guest_out.reshape(total_rows, HPD, ksplit, block_dims)
    state = (peaks, totals, outputs, guest_peak, guest_total, guest_out)
    for level in range(nbits):
        partner = from_partner(state, "ulys", level)
        state = merge_both(state, partner)
    own_out = lax.dynamic_index_in_dim(state[2], rank, 2, keepdims=False)
    guest_final = lax.dynamic_index_in_dim(state[5], rank, 2, keepdims=False)
    own_final = own_out / state[1][:, :, None]
    guest_final = guest_final / jnp.maximum(state[4], 1.0)[:, :, None]
    mixed = (own_final + guest_final).astype(jnp.bfloat16).reshape(total_rows, HPD * block_dims)
    proj_weight = out_weight[0]
    added = lax.psum_scatter(
        jnp.dot(mixed, proj_weight, preferred_element_type=jnp.float32).astype(jnp.bfloat16),
        "ulys",
        scatter_dimension=0,
        tiled=True,
    ).astype(jnp.float32)
    result = (lifted + modul[2] * added).astype(jnp.bfloat16)
    return passed_along(result[None], "pipe", 1)


LANES = 128
MIB = 1 << 20
VMEM = pl.BlockSpec(memory_space=pltpu.VMEM)
SMEM = pl.BlockSpec(memory_space=pltpu.SMEM)
HBM = pl.BlockSpec(memory_space=pltpu.HBM)


def in_hbm(x):
    return pltpu.with_memory_space_constraint(x, pltpu.HBM)


def limit(mib):
    return pltpu.CompilerParams(vmem_limit_bytes=mib * MIB)


def modulate_kernel(rows_ref, modul_ref, region_ref, block_ref, rows, modul, regions, sems):
    tokens, width = rows.shape
    copies = [
        pltpu.make_async_copy(source, target, sems.at[i])
        for i, (source, target) in enumerate(((rows_ref, rows), (modul_ref, modul), (region_ref, regions)))
    ]
    for copy in copies:
        copy.start()
    for copy in copies:
        copy.wait()
    lifted = rows[...].astype(jnp.float32)
    center = jnp.mean(lifted, axis=1, keepdims=True)
    spread = jnp.mean(jnp.square(lifted - center), axis=1, keepdims=True)
    normed = (lifted - center) * lax.rsqrt(spread + 1e-06)
    hidden = normed * (1.0 + modul[1]) + modul[0]
    block_ref[:, :width] = hidden.astype(jnp.bfloat16)
    square = (tokens, tokens)
    diagonal = lax.broadcasted_iota(jnp.int32, square, 0) == lax.broadcasted_iota(jnp.int32, square, 1)
    region = jnp.broadcast_to(regions[...].astype(jnp.float32), square)
    column = jnp.sum(jnp.where(diagonal, region, 0.0), axis=1, keepdims=True)
    block_ref[:, width:] = jnp.broadcast_to(column, (tokens, LANES)).astype(jnp.bfloat16)


def modulate(rows, modul, region):
    tokens, width = rows.shape
    return pl.pallas_call(
        modulate_kernel,
        out_shape=jax.ShapeDtypeStruct((tokens, width + LANES), jnp.bfloat16),
        in_specs=[HBM] * 3,
        out_specs=VMEM,
        scratch_shapes=[
            pltpu.VMEM(rows.shape, rows.dtype),
            pltpu.VMEM(modul.shape, modul.dtype),
            pltpu.VMEM(region.shape, region.dtype),
            pltpu.SemaphoreType.DMA((3,)),
        ],
        compiler_params=limit(8),
        name="modulate",
    )(*map(in_hbm, (rows, modul, region)))


def stage_kernel(head, chunk, cache_ref, guest_ref, weight_ref, proj_ref, *refs):
    keys_ref, values_ref, weight_out, proj_out, held, wide, sems = refs
    span, slots = cache_ref.shape[0], guest_ref.shape[0]
    lanes = pl.ds(head * HD, HD)
    spans = [(at, chunk, cache_ref.at[pl.ds(at, chunk), :, lanes]) for at in range(0, span, chunk)]
    spans.append((span, slots, guest_ref.at[:, :, lanes]))
    copies = [
        pltpu.make_async_copy(source, held.at[pl.ds(at, count)], sems.at[i])
        for i, (at, count, source) in enumerate(spans)
    ]
    columns = pl.ds(head * weight_out.shape[1], weight_out.shape[1])
    copies.append(pltpu.make_async_copy(weight_ref.at[:, columns], weight_out, sems.at[len(spans)]))
    rows = pl.ds(head * HD, HD)
    copies.append(pltpu.make_async_copy(proj_ref.at[rows], proj_out, sems.at[len(spans) + 1]))
    for copy in copies:
        copy.start()
    pairs = held.reshape(2 * held.shape[0], HD)
    for (first, count, _), copy in zip(spans, copies):
        copy.wait()
        for at in range(first, first + count, LANES):
            step = min(LANES, first + count - at)
            slot = wide.at[at // LANES % wide.shape[0]]
            slot[pl.ds(0, 2 * step), :] = pairs[pl.ds(2 * at, 2 * step), :].astype(jnp.float32)
            keys_ref[:, pl.ds(at, step)] = slot[pl.ds(0, step, stride=2), :].T.astype(jnp.bfloat16)
            values_ref[pl.ds(at, step), :] = slot[pl.ds(1, step, stride=2), :].astype(jnp.bfloat16)
    for copy in copies[len(spans) :]:
        copy.wait()


def stage(head, cache, guests, weight, proj):
    span, slots = cache.shape[0], guests.shape[0]
    total = span + slots
    pieces = 4
    shapes = [(HD, total), (total, HD), (weight.shape[0], HPD * HD), (HD, proj.shape[1])]
    moved = 2 * (3 * total * HD + weight.size // 3 + proj.size // 3)
    return pl.pallas_call(
        functools.partial(stage_kernel, head, span // pieces),
        out_shape=[jax.ShapeDtypeStruct(shape, jnp.bfloat16) for shape in shapes],
        in_specs=[HBM] * 4,
        out_specs=[VMEM] * 4,
        scratch_shapes=[
            pltpu.VMEM((total, 2, HD), jnp.bfloat16),
            pltpu.VMEM((4, 2 * LANES, HD), jnp.float32),
            pltpu.SemaphoreType.DMA((pieces + 3,)),
        ],
        compiler_params=limit(8),
        cost_estimate=pl.CostEstimate(flops=0, bytes_accessed=moved, transcendentals=0),
        name="stage",
    )(*map(in_hbm, (cache, guests, weight, proj)))


def project_kernel(parts, place, patch_ref, *refs):
    blocks, weights, stored = refs[:parts], refs[parts : parts + 3], refs[parts + 3 : parts + 3 + 2 * HPD]
    query_ref, region_ref, *fresh_refs = refs[parts + 3 + 2 * HPD : -1]
    rows = refs[-1]
    tokens = blocks[0].shape[0]
    total = parts * tokens
    width = weights[0].shape[0]
    for r in range(parts):
        rows[pl.ds(r * tokens, tokens)] = blocks[r][...]
    region_ref[...] = rows[:, width:]
    fresh = pl.ds(pl.multiple_of((2 * patch_ref[0] + place) * total, total), total)
    for kind in range(3):
        field = jnp.dot(rows[:, :width], weights[kind][...], preferred_element_type=jnp.float32)
        field = field.astype(jnp.bfloat16)
        if kind == 0:
            query_ref[...] = field
            continue
        for h in range(HPD):
            part = field[:, h * HD : (h + 1) * HD]
            if kind == 1:
                fresh_refs[2 * h][:, fresh] = part.T
            else:
                fresh_refs[2 * h + 1][fresh, :] = part


def project(place, patch, blocks, weights, stored):
    parts = len(blocks)
    tokens, wide = blocks[0].shape
    total = parts * tokens
    out_shape = [
        jax.ShapeDtypeStruct((total, HPD * HD), jnp.bfloat16),
        jax.ShapeDtypeStruct((total, LANES), jnp.bfloat16),
    ]
    out_shape += [jax.ShapeDtypeStruct(array.shape, array.dtype) for array in stored]
    first = 1 + parts + 3
    return pl.pallas_call(
        functools.partial(project_kernel, parts, place),
        out_shape=out_shape,
        in_specs=[SMEM] + [VMEM] * (parts + 3 + 2 * HPD),
        out_specs=[VMEM] * len(out_shape),
        scratch_shapes=[pltpu.VMEM((total, wide), jnp.bfloat16)],
        input_output_aliases={first + i: 2 + i for i in range(2 * HPD)},
        compiler_params=limit(8),
        cost_estimate=pl.CostEstimate(
            flops=2 * total * (wide - LANES) * 3 * HPD * HD, bytes_accessed=8 * MIB, transcendentals=0
        ),
        name="project",
    )(patch, *blocks, *weights, *stored)


def attend_kernel(order, outputs, counts_ref, modul_ref, *refs):
    queries, regions, refs = refs[:2], refs[2:4], refs[4:]
    stored, refs = refs[: 2 * HPD], refs[2 * HPD :]
    projs, refs = refs[:HPD], refs[HPD:]
    outs, refs = refs[: len(outputs)], refs[len(outputs) :]
    scores, mixed = refs[:HPD], refs[HPD]
    total, span = scores[0].shape
    tokens = total // len(order)
    width = projs[0].shape[1]
    slots = stored[0].shape[1] - span
    each = slots // SUBJ

    def rows_of(arrays, columns):
        half = arrays[0].shape[0] // tokens
        return jnp.concatenate(
            [arrays[r // half][pl.ds(r % half * tokens, tokens), columns] for r in order], axis=0
        )

    lane = lax.broadcasted_iota(jnp.int32, (1, slots), 1)
    code = jnp.full((1, slots), -1.0, jnp.float32)
    for s in range(SUBJ):
        live = (lane >= s * each) & (lane < s * each + counts_ref[0, s])
        code = jnp.where(live, s + 1.0, code)
    match = code == rows_of(regions, pl.ds(0, LANES))[:, :1].astype(jnp.float32)
    factor = HD ** (-0.5) * math.log2(math.e)
    query = [rows_of(queries, pl.ds(h * HD, HD)) for h in range(HPD)]
    chunk = 256
    tops = [None] * HPD

    def score(h, at):
        found = jnp.dot(query[h], stored[2 * h][:, pl.ds(at, chunk)], preferred_element_type=jnp.float32)
        scores[h][:, pl.ds(at, chunk)] = found
        both = jnp.maximum(found[:, :LANES], found[:, LANES:])
        tops[h] = both if tops[h] is None else jnp.maximum(tops[h], both)

    for at in range(0, span, chunk):
        score(0, at)
    for h in range(HPD):
        keys, values = stored[2 * h], stored[2 * h + 1]
        peak = jnp.max(tops[h], axis=1, keepdims=True) * factor
        found = jnp.dot(query[h], keys[:, span:], preferred_element_type=jnp.float32) * factor
        sums = own = None
        for at in range(0, span, chunk):
            if h + 1 < HPD:
                score(h + 1, at)
            raised = jnp.exp2(scores[h][:, pl.ds(at, chunk)] * factor - peak)
            both = raised[:, :LANES] + raised[:, LANES:]
            product = jnp.dot(
                raised.astype(jnp.bfloat16), values[pl.ds(at, chunk), :], preferred_element_type=jnp.float32
            )
            sums = both if sums is None else sums + both
            own = product if own is None else own + product
        own = own / jnp.sum(sums, axis=1, keepdims=True)
        peak = jnp.max(jnp.where(match, found, NEG_BIG), axis=1, keepdims=True)
        raised = jnp.where(match, jnp.exp2(jnp.where(match, found - peak, 0.0)), 0.0)
        guest = jnp.dot(raised.astype(jnp.bfloat16), values[span:, :], preferred_element_type=jnp.float32)
        guest = guest / jnp.maximum(jnp.sum(raised, axis=1, keepdims=True), 1.0)
        mixed[:, pl.ds(h * HD, HD)] = (own + guest).astype(jnp.bfloat16)
    for at in range(0, width, 512):
        columns = pl.ds(at, 512)
        proj = jnp.concatenate([share[:, columns] for share in projs], axis=0)
        part = jnp.dot(mixed[...], proj, preferred_element_type=jnp.float32) * modul_ref[2, :, columns]
        first = 0
        for out, count in zip(outs, outputs):
            terms = part[first : first + count * tokens]
            out[pl.ds(0, terms.shape[0]), columns] = terms.astype(out.dtype)
            first += count * tokens


def attend(order, outputs, tokens, span, counts, modul, queries, regions, stored, projs):
    total = len(order) * tokens
    width = projs[0].shape[1]
    return pl.pallas_call(
        functools.partial(attend_kernel, order, [count for count, _ in outputs]),
        out_shape=[jax.ShapeDtypeStruct((count * tokens, width), kind) for count, kind in outputs],
        in_specs=[SMEM] + [VMEM] * (5 + 3 * HPD),
        out_specs=[VMEM] * len(outputs),
        scratch_shapes=[pltpu.VMEM((total, span), jnp.float32)] * HPD
        + [pltpu.VMEM((total, HPD * HD), jnp.bfloat16)],
        compiler_params=limit(16),
        cost_estimate=pl.CostEstimate(
            flops=2 * total * HPD * HD * (width + 2 * span),
            bytes_accessed=16 * MIB,
            transcendentals=HPD * total * span,
        ),
        name="attend",
    )(counts, modul, *queries, *regions, *stored, *projs)


def add_kernel(kept_ref, *refs):
    total = kept_ref[...]
    for came_ref in refs[:-1]:
        total = total + came_ref[...].astype(jnp.float32)
    refs[-1][...] = total.astype(jnp.bfloat16)


def add_terms(kept, *came):
    return pl.pallas_call(
        add_kernel,
        out_shape=jax.ShapeDtypeStruct(kept.shape, jnp.bfloat16),
        in_specs=[VMEM] * (1 + len(came)),
        out_specs=VMEM,
        compiler_params=limit(4),
        name="add_terms",
    )(kept, *came)


def shards_whole(
    activations,
    patch_index,
    modulation,
    qkv_weight,
    out_weight,
    stale_cache,
    id_cache,
    region_ids,
    id_counts,
):
    pipes, group = lax.axis_size("pipe"), lax.axis_size("ulys")

    def beside(x, apart):
        return lax.ppermute(x, "ulys", [(i, i ^ apart) for i in range(group)])

    def onward(x, apart):
        pairs = [
            (p * group + i, (p + 1) % pipes * group + (i ^ apart))
            for p in range(pipes)
            for i in range(group)
        ]
        return lax.ppermute(x, ("pipe", "ulys"), pairs)

    hold = lax.optimization_barrier
    rows = activations[0]
    tokens = rows.shape[0]
    modul = modulation.transpose(1, 0, 2)
    stored = stale_cache[0, 0]
    guests = id_cache[0, 0]
    guests = guests.reshape(SUBJ * guests.shape[1], 2, HPD * HD)
    staged = functools.partial(stage, cache=stored, guests=guests, weight=qkv_weight[0], proj=out_weight[0])
    b0 = modulate(rows, modul, region_ids)
    b4, b1, b3, b2 = (beside(b0, r) for r in (4, 1, 3, 2))
    heads = [staged(h) for h in range(HPD)]
    b4, b1, *early = hold((b4, b1, *heads[0], *heads[1]))
    heads[0], heads[1] = early[: len(heads[0])], early[len(heads[0]) :]
    b7, b5, b6 = beside(b4, 3), beside(b4, 1), beside(b4, 2)
    weights, fields = [head[2] for head in heads], [array for head in heads for array in head[:2]]
    query_near, region_near, *fields = project(0, patch_index, (b0, b1, b2, b3), weights, fields)
    query_far, region_far, *fields = project(1, patch_index, (b4, b5, b6, b7), weights, fields)
    attended = functools.partial(
        attend,
        tokens=tokens,
        span=stored.shape[0],
        counts=id_counts,
        modul=modul,
        regions=(region_near, region_far),
        stored=fields,
        projs=[head[3] for head in heads],
    )
    narrow, wide = (1, jnp.bfloat16), (1, jnp.float32)
    t4, t7, t5, t6 = attended((4, 7, 5, 6), [wide] + [narrow] * 3, queries=(query_near, query_far))
    t4, t7, t5, t6, query_near = hold((t4, t7, t5, t6, query_near))
    t3, t1, t2, t0 = attended((3, 1, 2, 0), [narrow] * 4, queries=(query_near, query_far))
    t7, rows = hold((t7, rows))
    c7, c5, c6 = beside(t7, 3), beside(t5, 1), beside(t6, 2)
    before = onward(rows, 0)
    c3, c1, c2 = onward(t3, 3), onward(t1, 1), onward(t2, 2)
    s4 = add_terms(t4, c7, c5, c6)
    s4, t0 = hold((s4, t0))
    parts = before, c3, c1, c2, onward(s4, 4), onward(t0, 0)
    return sum(part.astype(jnp.float32) for part in parts).astype(jnp.bfloat16)[None]


def shards(*arrays):
    return (shards_whole if lax.axis_size("ulys") == GROUPS else shards_split)(*arrays)


def solution(mesh):
    placed = (
        P("pipe", "ulys", None),
        P("pipe"),
        P("pipe", None, None),
        P("pipe", None, "ulys"),
        P("pipe", "ulys", None),
        P("pipe", "ulys", None, None, None),
        P("pipe", "ulys", None, None, None, None),
        P("pipe", "ulys"),
        P("pipe", None),
    )
    return jax.shard_map(
        shards, mesh=mesh, in_specs=placed, out_specs=P("pipe", "ulys", None), check_vma=False
    )
```

```python
import functools
import math

import jax
import jax.numpy as jnp
from jax import lax
from jax.experimental import pallas as pl
from jax.experimental.pallas import tpu as pltpu
from jax.sharding import PartitionSpec as P

HD = 128
HPD = 3
GROUPS = 8
SUBJ = 6


NEG_BIG = -1e30


def as_sent(x):
    return jax.tree.map(lambda a: a.astype(jnp.bfloat16) if a.dtype == jnp.float32 else a, x)


def from_partner(x, axis, apart):
    return lax.ppermute(x, axis, [(i, i ^ 1 << apart) for i in range(lax.axis_size(axis))])


def passed_along(x, axis, by):
    size = lax.axis_size(axis)
    return lax.ppermute(x, axis, [(i, (i + by) % size) for i in range(size)])


def order_pair(mine, other, rank, level, axis):
    upper = rank // 2**level % 2
    first = jnp.where(upper == 1, other, mine)
    second = jnp.where(upper == 1, mine, other)
    return jnp.concatenate([first, second], axis=axis)


def block_attend(queries, keys, values, mask, factor):
    scores = jnp.einsum("qhd,khd->qhk", queries, keys, preferred_element_type=jnp.float32) * factor
    if mask is None:
        peak = jnp.max(scores, axis=2)
        weights = jnp.exp(scores - peak[:, :, None])
    else:
        wide = mask[:, None, :]
        peak = jnp.max(jnp.where(wide, scores, NEG_BIG), axis=2)
        weights = jnp.where(wide, jnp.exp(jnp.where(wide, scores - peak[:, :, None], 0.0)), 0.0)
    total = jnp.sum(weights, axis=2)
    output = jnp.einsum(
        "qhk,khd->qhd", weights.astype(jnp.bfloat16), values, preferred_element_type=jnp.float32
    )
    return (peak, total, output)


def merge_parts(first, second):
    peak = jnp.maximum(first[0], second[0])
    weight_one = jnp.exp(first[0] - peak)
    weight_two = jnp.exp(second[0] - peak)
    total = first[1] * weight_one + second[1] * weight_two
    output = first[2] * weight_one[:, :, None, None] + second[2] * weight_two[:, :, None, None]
    return (peak, total, output)


def merge_both(first, second):
    return merge_parts(first[:3], second[:3]) + merge_parts(first[3:], second[3:])


def shards_split(
    activations,
    patch_index,
    modulation,
    qkv_weight,
    out_weight,
    stale_cache,
    id_cache,
    region_ids,
    id_counts,
):
    ksplit = lax.axis_size("ulys") // GROUPS
    nbits = ksplit.bit_length() - 1
    rank = lax.axis_index("ulys") % ksplit
    rows = activations[0]
    modul = modulation[0]
    lifted = rows.astype(jnp.float32)
    center = jnp.mean(lifted, axis=1, keepdims=True)
    spread = jnp.mean(jnp.square(lifted - center), axis=1, keepdims=True)
    normed = (lifted - center) * lax.rsqrt(spread + 1e-06)
    hidden = (normed * (1.0 + modul[1]) + modul[0]).astype(jnp.bfloat16)
    all_rows, all_regions = (
        lax.all_gather(hidden, "ulys", axis=0, tiled=True),
        lax.all_gather(region_ids[0].astype(jnp.bfloat16), "ulys", axis=0, tiled=True),
    )
    total_rows = all_rows.shape[0]
    weight = qkv_weight[0]
    block_dims = HD // ksplit
    pieces = jnp.dot(all_rows, weight, preferred_element_type=jnp.float32).astype(jnp.bfloat16)[
        :, None, :
    ]
    for level in range(nbits):
        partner = from_partner(as_sent(pieces), "ulys", level).astype(pieces.dtype)
        pieces = order_pair(pieces, partner, rank, level, 1)
    fields = (
        pieces.reshape(total_rows, ksplit, 3, HPD, block_dims)
        .transpose(2, 0, 3, 1, 4)
        .reshape(3, total_rows, HPD, HD)
    )
    queries = fields[0]
    stored = stale_cache[0, 0]
    span = stored.shape[0]
    old_keys = stored[:, 0].reshape(span, HPD, HD)
    old_values = stored[:, 1].reshape(span, HPD, HD)
    patch = patch_index[0]
    per_block = span // total_rows
    owner = patch // per_block
    offset = patch % per_block * total_rows
    keys = jnp.where(
        rank == owner, lax.dynamic_update_slice(old_keys, fields[1], (offset, 0, 0)), old_keys
    )
    values = jnp.where(
        rank == owner, lax.dynamic_update_slice(old_values, fields[2], (offset, 0, 0)), old_values
    )
    factor = HD ** (-0.5)
    query_block = min(512, total_rows)
    block_count = total_rows // query_block

    def attend_rows(query_rows):
        return block_attend(query_rows, keys, values, None, factor)

    peaks, totals, outputs = lax.map(
        attend_rows, queries.reshape(block_count, query_block, HPD, HD)
    )
    peaks = peaks.reshape(total_rows, HPD)
    totals = totals.reshape(total_rows, HPD)
    outputs = outputs.reshape(total_rows, HPD, ksplit, block_dims)
    guests = id_cache[0, 0]
    id_slots = guests.shape[1]
    guest_keys = guests[:, :, 0].reshape(SUBJ * id_slots, HPD, HD)
    guest_values = guests[:, :, 1].reshape(SUBJ * id_slots, HPD, HD)
    slot_index = jnp.arange(id_slots, dtype=jnp.int32) + rank * id_slots
    valid = slot_index[None, :] < id_counts[0][:, None]
    subject = jnp.arange(1, SUBJ + 1).astype(jnp.bfloat16)
    match = all_regions[:, None] == subject[None, :]
    mask = (match[:, :, None] & valid[None]).reshape(total_rows, SUBJ * id_slots)
    guest_peak, guest_total, guest_out = block_attend(
        queries, guest_keys, guest_values, mask, factor
    )
    guest_out = guest_out.reshape(total_rows, HPD, ksplit, block_dims)
    state = (peaks, totals, outputs, guest_peak, guest_total, guest_out)
    for level in range(nbits):
        partner = from_partner(state, "ulys", level)
        state = merge_both(state, partner)
    own_out = lax.dynamic_index_in_dim(state[2], rank, 2, keepdims=False)
    guest_final = lax.dynamic_index_in_dim(state[5], rank, 2, keepdims=False)
    own_final = own_out / state[1][:, :, None]
    guest_final = guest_final / jnp.maximum(state[4], 1.0)[:, :, None]
    mixed = (own_final + guest_final).astype(jnp.bfloat16).reshape(total_rows, HPD * block_dims)
    proj_weight = out_weight[0]
    added = lax.psum_scatter(
        jnp.dot(mixed, proj_weight, preferred_element_type=jnp.float32).astype(jnp.bfloat16),
        "ulys",
        scatter_dimension=0,
        tiled=True,
    ).astype(jnp.float32)
    result = (lifted + modul[2] * added).astype(jnp.bfloat16)
    return passed_along(result[None], "pipe", 1)


LANES = 128
MIB = 1 << 20
VMEM = pl.BlockSpec(memory_space=pltpu.VMEM)
SMEM = pl.BlockSpec(memory_space=pltpu.SMEM)
HBM = pl.BlockSpec(memory_space=pltpu.HBM)


def in_hbm(x):
    return pltpu.with_memory_space_constraint(x, pltpu.HBM)


def limit(mib):
    return pltpu.CompilerParams(vmem_limit_bytes=mib * MIB)


def modulate_kernel(rows_ref, modul_ref, region_ref, block_ref, rows, modul, regions, sems):
    tokens, width = rows.shape
    copies = [
        pltpu.make_async_copy(source, target, sems.at[i])
        for i, (source, target) in enumerate(((rows_ref, rows), (modul_ref, modul), (region_ref, regions)))
    ]
    for copy in copies:
        copy.start()
    for copy in copies:
        copy.wait()
    lifted = rows[...].astype(jnp.float32)
    center = jnp.mean(lifted, axis=1, keepdims=True)
    spread = jnp.mean(jnp.square(lifted - center), axis=1, keepdims=True)
    normed = (lifted - center) * lax.rsqrt(spread + 1e-06)
    hidden = normed * (1.0 + modul[1]) + modul[0]
    block_ref[:, :width] = hidden.astype(jnp.bfloat16)
    square = (tokens, tokens)
    diagonal = lax.broadcasted_iota(jnp.int32, square, 0) == lax.broadcasted_iota(jnp.int32, square, 1)
    region = jnp.broadcast_to(regions[...].astype(jnp.float32), square)
    column = jnp.sum(jnp.where(diagonal, region, 0.0), axis=1, keepdims=True)
    block_ref[:, width:] = jnp.broadcast_to(column, (tokens, LANES)).astype(jnp.bfloat16)


def modulate(rows, modul, region):
    tokens, width = rows.shape
    return pl.pallas_call(
        modulate_kernel,
        out_shape=jax.ShapeDtypeStruct((tokens, width + LANES), jnp.bfloat16),
        in_specs=[HBM] * 3,
        out_specs=VMEM,
        scratch_shapes=[
            pltpu.VMEM(rows.shape, rows.dtype),
            pltpu.VMEM(modul.shape, modul.dtype),
            pltpu.VMEM(region.shape, region.dtype),
            pltpu.SemaphoreType.DMA((3,)),
        ],
        compiler_params=limit(8),
        name="modulate",
    )(*map(in_hbm, (rows, modul, region)))


def stage_kernel(head, chunk, cache_ref, guest_ref, weight_ref, proj_ref, *refs):
    keys_ref, values_ref, weight_out, proj_out, held, wide, sems = refs
    span, slots = cache_ref.shape[0], guest_ref.shape[0]
    lanes = pl.ds(head * HD, HD)
    spans = [(at, chunk, cache_ref.at[pl.ds(at, chunk), :, lanes]) for at in range(0, span, chunk)]
    spans.append((span, slots, guest_ref.at[:, :, lanes]))
    copies = [
        pltpu.make_async_copy(source, held.at[pl.ds(at, count)], sems.at[i])
        for i, (at, count, source) in enumerate(spans)
    ]
    columns = pl.ds(head * weight_out.shape[1], weight_out.shape[1])
    copies.append(pltpu.make_async_copy(weight_ref.at[:, columns], weight_out, sems.at[len(spans)]))
    rows = pl.ds(head * HD, HD)
    copies.append(pltpu.make_async_copy(proj_ref.at[rows], proj_out, sems.at[len(spans) + 1]))
    for copy in copies:
        copy.start()
    pairs = held.reshape(2 * held.shape[0], HD)
    for (first, count, _), copy in zip(spans, copies):
        copy.wait()
        for at in range(first, first + count, LANES):
            step = min(LANES, first + count - at)
            slot = wide.at[at // LANES % wide.shape[0]]
            slot[pl.ds(0, 2 * step), :] = pairs[pl.ds(2 * at, 2 * step), :].astype(jnp.float32)
            keys_ref[:, pl.ds(at, step)] = slot[pl.ds(0, step, stride=2), :].T.astype(jnp.bfloat16)
            values_ref[pl.ds(at, step), :] = slot[pl.ds(1, step, stride=2), :].astype(jnp.bfloat16)
    for copy in copies[len(spans) :]:
        copy.wait()


def stage(head, cache, guests, weight, proj):
    span, slots = cache.shape[0], guests.shape[0]
    total = span + slots
    pieces = 4
    shapes = [(HD, total), (total, HD), (weight.shape[0], HPD * HD), (HD, proj.shape[1])]
    moved = 2 * (3 * total * HD + weight.size // 3 + proj.size // 3)
    return pl.pallas_call(
        functools.partial(stage_kernel, head, span // pieces),
        out_shape=[jax.ShapeDtypeStruct(shape, jnp.bfloat16) for shape in shapes],
        in_specs=[HBM] * 4,
        out_specs=[VMEM] * 4,
        scratch_shapes=[
            pltpu.VMEM((total, 2, HD), jnp.bfloat16),
            pltpu.VMEM((4, 2 * LANES, HD), jnp.float32),
            pltpu.SemaphoreType.DMA((pieces + 3,)),
        ],
        compiler_params=limit(8),
        cost_estimate=pl.CostEstimate(flops=0, bytes_accessed=moved, transcendentals=0),
        name="stage",
    )(*map(in_hbm, (cache, guests, weight, proj)))


def project_kernel(parts, place, patch_ref, *refs):
    blocks, weights, stored = refs[:parts], refs[parts : parts + 3], refs[parts + 3 : parts + 3 + 2 * HPD]
    query_ref, region_ref, *fresh_refs = refs[parts + 3 + 2 * HPD : -1]
    rows = refs[-1]
    tokens = blocks[0].shape[0]
    total = parts * tokens
    width = weights[0].shape[0]
    for r in range(parts):
        rows[pl.ds(r * tokens, tokens)] = blocks[r][...]
    region_ref[...] = rows[:, width:]
    fresh = pl.ds(pl.multiple_of((2 * patch_ref[0] + place) * total, total), total)
    for kind in range(3):
        field = jnp.dot(rows[:, :width], weights[kind][...], preferred_element_type=jnp.float32)
        field = field.astype(jnp.bfloat16)
        if kind == 0:
            query_ref[...] = field
            continue
        for h in range(HPD):
            part = field[:, h * HD : (h + 1) * HD]
            if kind == 1:
                fresh_refs[2 * h][:, fresh] = part.T
            else:
                fresh_refs[2 * h + 1][fresh, :] = part


def project(place, patch, blocks, weights, stored):
    parts = len(blocks)
    tokens, wide = blocks[0].shape
    total = parts * tokens
    out_shape = [
        jax.ShapeDtypeStruct((total, HPD * HD), jnp.bfloat16),
        jax.ShapeDtypeStruct((total, LANES), jnp.bfloat16),
    ]
    out_shape += [jax.ShapeDtypeStruct(array.shape, array.dtype) for array in stored]
    first = 1 + parts + 3
    return pl.pallas_call(
        functools.partial(project_kernel, parts, place),
        out_shape=out_shape,
        in_specs=[SMEM] + [VMEM] * (parts + 3 + 2 * HPD),
        out_specs=[VMEM] * len(out_shape),
        scratch_shapes=[pltpu.VMEM((total, wide), jnp.bfloat16)],
        input_output_aliases={first + i: 2 + i for i in range(2 * HPD)},
        compiler_params=limit(8),
        cost_estimate=pl.CostEstimate(
            flops=2 * total * (wide - LANES) * 3 * HPD * HD, bytes_accessed=8 * MIB, transcendentals=0
        ),
        name="project",
    )(patch, *blocks, *weights, *stored)


def attend_kernel(order, outputs, counts_ref, modul_ref, *refs):
    queries, regions, refs = refs[:2], refs[2:4], refs[4:]
    stored, refs = refs[: 2 * HPD], refs[2 * HPD :]
    projs, refs = refs[:HPD], refs[HPD:]
    outs, refs = refs[: len(outputs)], refs[len(outputs) :]
    scores, mixed = refs[:HPD], refs[HPD]
    total, span = scores[0].shape
    tokens = total // len(order)
    width = projs[0].shape[1]
    slots = stored[0].shape[1] - span
    each = slots // SUBJ

    def rows_of(arrays, columns):
        half = arrays[0].shape[0] // tokens
        return jnp.concatenate(
            [arrays[r // half][pl.ds(r % half * tokens, tokens), columns] for r in order], axis=0
        )

    lane = lax.broadcasted_iota(jnp.int32, (1, slots), 1)
    code = jnp.full((1, slots), -1.0, jnp.float32)
    for s in range(SUBJ):
        live = (lane >= s * each) & (lane < s * each + counts_ref[0, s])
        code = jnp.where(live, s + 1.0, code)
    match = code == rows_of(regions, pl.ds(0, LANES))[:, :1].astype(jnp.float32)
    factor = HD ** (-0.5) * math.log2(math.e)
    query = [rows_of(queries, pl.ds(h * HD, HD)) for h in range(HPD)]
    chunk = 256
    tops = [None] * HPD

    def score(h, at):
        found = jnp.dot(query[h], stored[2 * h][:, pl.ds(at, chunk)], preferred_element_type=jnp.float32)
        scores[h][:, pl.ds(at, chunk)] = found
        both = jnp.maximum(found[:, :LANES], found[:, LANES:])
        tops[h] = both if tops[h] is None else jnp.maximum(tops[h], both)

    for at in range(0, span, chunk):
        score(0, at)
    for h in range(HPD):
        keys, values = stored[2 * h], stored[2 * h + 1]
        peak = jnp.max(tops[h], axis=1, keepdims=True) * factor
        found = jnp.dot(query[h], keys[:, span:], preferred_element_type=jnp.float32) * factor
        sums = own = None
        for at in range(0, span, chunk):
            if h + 1 < HPD:
                score(h + 1, at)
            raised = jnp.exp2(scores[h][:, pl.ds(at, chunk)] * factor - peak)
            both = raised[:, :LANES] + raised[:, LANES:]
            product = jnp.dot(
                raised.astype(jnp.bfloat16), values[pl.ds(at, chunk), :], preferred_element_type=jnp.float32
            )
            sums = both if sums is None else sums + both
            own = product if own is None else own + product
        own = own / jnp.sum(sums, axis=1, keepdims=True)
        peak = jnp.max(jnp.where(match, found, NEG_BIG), axis=1, keepdims=True)
        raised = jnp.where(match, jnp.exp2(jnp.where(match, found - peak, 0.0)), 0.0)
        guest = jnp.dot(raised.astype(jnp.bfloat16), values[span:, :], preferred_element_type=jnp.float32)
        guest = guest / jnp.maximum(jnp.sum(raised, axis=1, keepdims=True), 1.0)
        mixed[:, pl.ds(h * HD, HD)] = (own + guest).astype(jnp.bfloat16)
    for at in range(0, width, 512):
        columns = pl.ds(at, 512)
        proj = jnp.concatenate([share[:, columns] for share in projs], axis=0)
        part = jnp.dot(mixed[...], proj, preferred_element_type=jnp.float32) * modul_ref[2, :, columns]
        first = 0
        for out, count in zip(outs, outputs):
            terms = part[first : first + count * tokens]
            out[pl.ds(0, terms.shape[0]), columns] = terms.astype(out.dtype)
            first += count * tokens


def attend(order, outputs, tokens, span, counts, modul, queries, regions, stored, projs):
    total = len(order) * tokens
    width = projs[0].shape[1]
    return pl.pallas_call(
        functools.partial(attend_kernel, order, [count for count, _ in outputs]),
        out_shape=[jax.ShapeDtypeStruct((count * tokens, width), kind) for count, kind in outputs],
        in_specs=[SMEM] + [VMEM] * (5 + 3 * HPD),
        out_specs=[VMEM] * len(outputs),
        scratch_shapes=[pltpu.VMEM((total, span), jnp.float32)] * HPD
        + [pltpu.VMEM((total, HPD * HD), jnp.bfloat16)],
        compiler_params=limit(16),
        cost_estimate=pl.CostEstimate(
            flops=2 * total * HPD * HD * (width + 2 * span),
            bytes_accessed=16 * MIB,
            transcendentals=HPD * total * span,
        ),
        name="attend",
    )(counts, modul, *queries, *regions, *stored, *projs)


def add_kernel(kept_ref, *refs):
    total = kept_ref[...]
    for came_ref in refs[:-1]:
        total = total + came_ref[...].astype(jnp.float32)
    refs[-1][...] = total.astype(jnp.bfloat16)


def add_terms(kept, *came):
    return pl.pallas_call(
        add_kernel,
        out_shape=jax.ShapeDtypeStruct(kept.shape, jnp.bfloat16),
        in_specs=[VMEM] * (1 + len(came)),
        out_specs=VMEM,
        compiler_params=limit(4),
        name="add_terms",
    )(kept, *came)


def shards_whole(
    activations,
    patch_index,
    modulation,
    qkv_weight,
    out_weight,
    stale_cache,
    id_cache,
    region_ids,
    id_counts,
):
    pipes, group = lax.axis_size("pipe"), lax.axis_size("ulys")

    def beside(x, apart):
        return lax.ppermute(x, "ulys", [(i, i ^ apart) for i in range(group)])

    def onward(x, apart):
        pairs = [
            (p * group + i, (p + 1) % pipes * group + (i ^ apart))
            for p in range(pipes)
            for i in range(group)
        ]
        return lax.ppermute(x, ("pipe", "ulys"), pairs)

    hold = lax.optimization_barrier
    rows = activations[0]
    tokens = rows.shape[0]
    modul = modulation.transpose(1, 0, 2)
    stored = stale_cache[0, 0]
    guests = id_cache[0, 0]
    guests = guests.reshape(SUBJ * guests.shape[1], 2, HPD * HD)
    staged = functools.partial(stage, cache=stored, guests=guests, weight=qkv_weight[0], proj=out_weight[0])
    b0 = modulate(rows, modul, region_ids)
    b4, b1, b3, b2 = (beside(b0, r) for r in (4, 1, 3, 2))
    heads = [staged(h) for h in range(HPD)]
    b4, *early = hold((b4, *heads[0], *heads[1]))
    heads[0], heads[1] = early[: len(heads[0])], early[len(heads[0]) :]
    b7, b5, b6 = beside(b4, 3), beside(b4, 1), beside(b4, 2)
    weights, fields = [head[2] for head in heads], [array for head in heads for array in head[:2]]
    query_near, region_near, *fields = project(0, patch_index, (b0, b1, b2, b3), weights, fields)
    query_far, region_far, *fields = project(1, patch_index, (b4, b5, b6, b7), weights, fields)
    attended = functools.partial(
        attend,
        tokens=tokens,
        span=stored.shape[0],
        counts=id_counts,
        modul=modul,
        regions=(region_near, region_far),
        stored=fields,
        projs=[head[3] for head in heads],
    )
    narrow, wide = (1, jnp.bfloat16), (1, jnp.float32)
    t4, t7, t5, t6 = attended((4, 7, 5, 6), [wide] + [narrow] * 3, queries=(query_near, query_far))
    t4, t7, t5, t6, query_near = hold((t4, t7, t5, t6, query_near))
    t3, t1, t2, t0 = attended((3, 1, 2, 0), [narrow] * 4, queries=(query_near, query_far))
    c7, c5, c6 = beside(t7, 3), beside(t5, 1), beside(t6, 2)
    rows, t3, t1, t2, t0 = hold((rows, t3, t1, t2, t0))
    before = onward(rows, 0)
    c3, c1 = onward(t3, 3), onward(t1, 1)
    s4 = add_terms(t4, c7, c5, c6)
    s4, t0, t2 = hold((s4, t0, t2))
    parts = before, c3, c1, onward(s4, 4), onward(t2, 2), onward(t0, 0)
    return sum(part.astype(jnp.float32) for part in parts).astype(jnp.bfloat16)[None]


def shards(*arrays):
    return (shards_whole if lax.axis_size("ulys") == GROUPS else shards_split)(*arrays)


def solution(mesh):
    placed = (
        P("pipe", "ulys", None),
        P("pipe"),
        P("pipe", None, None),
        P("pipe", None, "ulys"),
        P("pipe", "ulys", None),
        P("pipe", "ulys", None, None, None),
        P("pipe", "ulys", None, None, None, None),
        P("pipe", "ulys"),
        P("pipe", None),
    )
    return jax.shard_map(
        shards, mesh=mesh, in_specs=placed, out_specs=P("pipe", "ulys", None), check_vma=False
    )
```
